32 devices in a mesh: chan: 4 (over z), win: 8 (over y, x, core).
Axes of the slice: x: 2, y: 2, z: 4, core: 2. Of those that a mesh axis runs over, the one named last changes fastest.
Arguments:
- spectra: bfloat16 [2, 128, 128, 384], P(None, 'win', 'chan'), may hold values from -6 to 6
- valid: int32 [128, 128], P('win', 'chan'), may hold values 0 or 1
- source_block: int32 [4], replicated, may hold values from 0 to 3, as said below
Outputs:
- linear_stack: float32 [128, 128, 1024], P('win', 'chan')
- phase_weighted: float32 [128, 128, 1024], P('win', 'chan')
The draws below stay inside these ranges and needn't reach their ends.
Inputs may be any that keep to these rules, and one draw needn't show every extreme that they name: The entries of source_block are distinct group numbers; group g holds the channels g * 32 up to g * 32 + 31.
All inputs are finite; a program needn't handle non-finite values. No bound on the sum of `valid` on one device may be relied on, other than what follows from the above.
Results may differ from the reference program's by a relative error of at most 0.00032.
Values may be sent and summed in bfloat16 or wider, within the bound.
No kernel may reach another device: no remote copies, remote signals or barrier semaphores. Data moves between devices by JAX's collectives and lax.ppermute only.
A program may use at most 128 MiB of HBM per device.

```python
import math
import jax
import jax.numpy as jnp
from jax import lax

FREQ = 384
LAGS = 1024
SRC_W = 128
CH_DEV = 32
WINDOWS = 128
CHANNELS = 128


def draw_source_block(key, part):
    order = jax.random.permutation(jax.random.fold_in(key, 17), CHANNELS // CH_DEV)
    return order[:SRC_W // CH_DEV].astype(jnp.int32)


def draw_spectra(key, part):
    key = jax.random.fold_in(key, 5)
    noise_key, common_key, alive_key = jax.random.split(key, 3)
    full_shape = (2, WINDOWS, CHANNELS, FREQ)
    noise_part = jax.random.normal(noise_key, full_shape, jnp.float32)
    strength = 0.8
    common = jax.random.normal(common_key, (2, WINDOWS, 1, FREQ), jnp.float32)
    channel_index = jnp.arange(CHANNELS, dtype=jnp.int32)
    delays = channel_index * (LAGS * 9 // 20) // CHANNELS
    freq_bins = 60 + jnp.arange(FREQ, dtype=jnp.int32)
    angles = jnp.mod(delays[:, None] * freq_bins[None, :], 15000).astype(jnp.float32) * (2.0 * math.pi / 15000.0)
    cos_part = jnp.cos(angles)[None]
    sin_part = jnp.sin(angles)[None]
    rotated_re = common[0] * cos_part - common[1] * sin_part
    rotated_im = common[0] * sin_part + common[1] * cos_part
    coherent = jnp.stack([rotated_re, rotated_im])
    alive_rows = jax.random.bernoulli(alive_key, 0.75, (1, WINDOWS, CHANNELS, 1)).astype(jnp.float32)
    values = jnp.clip(noise_part + strength * coherent, -6.0, 6.0) * alive_rows
    return values.astype(jnp.bfloat16)


def touch_ends(entries, stream_key, low, top_value):
    longest = entries.shape.index(max(entries.shape))
    spots = []
    for shift in (0, 1):
        where = [jax.random.randint(jax.random.fold_in(stream_key, axis), (), 0, length) for axis, length in enumerate(entries.shape)]
        where[longest] = (where[longest] + shift) % entries.shape[longest]
        spots.append(tuple(where))
    return entries.at[spots[0]].set(low).at[spots[1]].set(top_value)


def setup_inputs(seed: int = 0) -> dict:
    splits = jax.random.split(jax.random.key(seed), 4)
    return {
        "spectra": draw_spectra(jax.random.fold_in(splits[3], 71), 0),
        "valid": touch_ends((jax.random.randint(splits[1], (WINDOWS, CHANNELS), 0, 8) < 7).astype(jnp.int32), jax.random.fold_in(splits[1], 1), 0, 1),
        "source_block": draw_source_block(jax.random.fold_in(splits[3], 71), 0),
    }


lowest_bin = 60
window_samples = 15000
amp_eps = 1e-05
phase_floor = 0.5

def prepare(spectra, valid):
    real_part = spectra[0].astype(jnp.float32)
    imag_part = spectra[1].astype(jnp.float32)
    power = real_part * real_part + imag_part * imag_part
    scale_amp = jnp.sqrt(lax.optimization_barrier(jnp.mean(power, axis=-1, keepdims=True)) + amp_eps)
    weight = valid.astype(jnp.float32)[:, :, None]
    paired = jnp.stack([real_part, imag_part])
    white = (paired * (weight / scale_amp)).astype(jnp.bfloat16)
    unit = (paired * (weight / jnp.maximum(jnp.sqrt(power), phase_floor))).astype(jnp.bfloat16)
    return (white, unit)

def lag_table(freq, lags):
    bins = lowest_bin + jnp.arange(freq, dtype=jnp.int32)
    shifts = jnp.arange(lags, dtype=jnp.int32) - lags // 2
    phase = jnp.mod(bins[:, None] * shifts[None, :], window_samples)
    theta = phase.astype(jnp.float32) * (2.0 * math.pi / window_samples)
    return jnp.concatenate([jnp.cos(theta), jnp.sin(theta)], axis=0)

def cross(source, receiver):
    source = source.astype(jnp.float32)
    receiver = receiver.astype(jnp.float32)
    turned = jnp.stack([receiver[1], -receiver[0]])
    real_sum = jnp.einsum('kwsf,kwrf->srf', source, receiver)
    imag_sum = jnp.einsum('kwsf,kwrf->srf', source, turned)
    return (real_sum, imag_sum)

def finish(rows, counts, table, windows, freq):
    den = jnp.maximum(counts, 1.0)[:, :, None]
    mean_re = rows[:, 0] / den
    mean_im = rows[:, 1] / den
    coher = (rows[:, 2] * rows[:, 2] + rows[:, 3] * rows[:, 3]) / (den * den)
    linear_part = jnp.concatenate([mean_re, -mean_im], axis=-1)
    weighted = linear_part * jnp.concatenate([coher, coher], axis=-1)
    both = jnp.stack([linear_part, weighted])
    shape = both.shape
    lagged = jnp.dot(both.reshape(-1, shape[-1]), table, precision=lax.Precision.HIGHEST, preferred_element_type=jnp.float32).reshape(shape[0], shape[1], shape[2], -1)
    factor = math.sqrt(windows / freq)
    return (lagged[0] * factor, lagged[1] * (factor * windows))

def reference(spectra, valid, source_block):
    white, unit = prepare(spectra, valid)
    chosen = (source_block[:, None].astype(jnp.int32) * CH_DEV + jnp.arange(CH_DEV, dtype=jnp.int32)[None, :]).reshape(-1)
    src_white = jnp.take(white, chosen, axis=2)
    src_unit = jnp.take(unit, chosen, axis=2)
    maskf = valid.astype(jnp.float32)
    src_mask = jnp.take(maskf, chosen, axis=1)
    lin_re, lin_im = cross(src_white, white)
    pha_re, pha_im = cross(src_unit, unit)
    rows = jnp.stack([lin_re, lin_im, pha_re, pha_im], axis=1)
    counts = jnp.einsum('ws,wr->sr', src_mask, maskf)
    table = lag_table(FREQ, LAGS)
    return finish(rows, counts, table, WINDOWS, FREQ)
```

```python
import functools
import math

import jax
import jax.numpy as jnp
import ml_dtypes
import numpy as np
from jax import lax
from jax.experimental import pallas as pl
from jax.experimental.pallas import tpu as pltpu
from jax.sharding import PartitionSpec as P

LAGS = 1024
SRC_W = 128

lowest_bin = 60
window_samples = 15000
amp_eps = 1e-05
phase_floor = 0.5

PACK = 4
CHUNKS = (1.0,)
VMEM = 60 * 1024 * 1024


def chunk_sizes(slots):
    edges = [0]
    total = 0.0
    for share in CHUNKS:
        total += share
        edges.append(round(slots * total))
    return [edges[i + 1] - edges[i] for i in range(len(CHUNKS))]


def pack_kernel(sizes, devs, spectra_ref, valid_ref, *rest):
    outs, (wide, turned) = rest[: len(sizes)], rest[len(sizes) :]
    kinds, windows, chans, freq = spectra_ref.shape
    span = freq // PACK
    slots = span // devs
    real_part = spectra_ref[0].astype(jnp.float32)
    imag_part = spectra_ref[1].astype(jnp.float32)
    for i in range(freq // 128):
        cut = slice(i * 128, (i + 1) * 128)
        wide[i, pl.ds(0, windows * chans), :] = real_part[:, :, cut].reshape(windows * chans, 128)
        wide[i, pl.ds(windows * chans, windows * chans), :] = imag_part[:, :, cut].reshape(windows * chans, 128)
    total = jnp.sum(real_part * real_part + imag_part * imag_part, axis=-1, keepdims=True)
    lane = lax.broadcasted_iota(jnp.int32, (chans, 128), 1)
    energy = jnp.zeros((chans, 128), jnp.float32)
    for w in range(windows):
        energy = jnp.where(lane % windows == w, total[w], energy)
    scale = valid_ref[...] / jnp.sqrt(energy * (1.0 / freq) + amp_eps)
    high = scale.astype(jnp.bfloat16).astype(jnp.float32)
    middle = (scale - high).astype(jnp.bfloat16).astype(jnp.float32)
    low = scale - high - middle
    part = lane // windows
    split = jnp.where(part == 0, high, jnp.where(part == 1, middle, jnp.where(part == 2, low, 0.0)))
    for c in range(chans):
        rows = []
        for k in range(kinds):
            rows_at = pl.ds(k * windows * chans + c, windows, stride=chans)
            line = jnp.concatenate([wide[i, rows_at, :] for i in range(freq // 128)], axis=1)
            for b in range(PACK):
                moved = line if b == 0 else pltpu.roll(line, freq - b * span, 1)
                rows.append(moved[:, :128])
        flipped = jnp.concatenate(rows, axis=0).T
        turned[pl.ds(c, span, stride=chans), :] = flipped[:span]
    for d in range(devs):
        start = d * slots
        for i, out in enumerate(outs):
            block = turned[pl.ds(start * chans, sizes[i] * chans), :]
            out[d, : sizes[i]] = block.astype(jnp.bfloat16).reshape(sizes[i], chans, 128)
            if i == 0:
                out[d, sizes[0]] = split.astype(jnp.bfloat16)
            start += sizes[i]


def swap_blocks(arrays, width):
    arrays = list(arrays)
    lane = lax.broadcasted_iota(jnp.int32, arrays[0].shape, 1)
    bit = 1
    while bit < len(arrays):
        upper = (lane // (width * bit)) % 2 == 1
        for i in range(len(arrays)):
            if i & bit == 0:
                a, c = arrays[i], arrays[i | bit]
                arrays[i] = jnp.where(upper, pltpu.roll(c, width * bit, 1), a)
                arrays[i | bit] = jnp.where(upper, c, pltpu.roll(a, 128 - width * bit, 1))
        bit *= 2
    return arrays


def cross_kernel(groups, own_first, pos_ref, *rest):
    blocks = rest[:groups]
    rest = rest[groups:]
    own = blocks[0]
    if not own_first:
        own, rest = rest[0], rest[1:]
    scales = rest[:groups]
    rest = rest[groups:]
    own_scale = scales[0]
    if not own_first:
        own_scale, rest = rest[0], rest[1:]
    out, factor, cap, src_white, src_unit, recv_white, recv_unit, inv = rest
    devs, chans = own_scale.shape[0], own_scale.shape[2]
    width = 128 // 8
    parts = devs // 8
    half = parts * 128
    slots = out.shape[1] // PACK
    rows_out = out.shape[2]
    per_group = chans // rows_out
    sets = groups if own_first else groups + 1

    def opened(ref, q, part):
        return swap_blocks([ref[part * 8 + d, q].astype(jnp.float32) for d in range(8)], width)

    scale_refs = list(scales) if own_first else list(scales) + [own_scale]
    for g, ref in enumerate(scale_refs):
        for part in range(parts):
            got = opened(ref, 0, part)
            value = got[0] + got[1] + got[2]
            factor[pl.ds(g * chans, chans), pl.ds(part * 128, 128)] = value
            cap[pl.ds(g * chans, chans), pl.ds(part * 128, 128)] = jnp.where(value > 0, 1.0 / phase_floor, 0.0)
    masks = jnp.where(cap[...] > 0, 1.0, 0.0).astype(jnp.bfloat16)
    mine = 0 if own_first else groups * chans
    recv = jnp.concatenate([masks[mine : mine + chans]] * 4, axis=0)
    counts = lax.dot_general(
        masks[: groups * chans], recv, (((1,), (1,)), ((), ())), preferred_element_type=jnp.float32
    )
    inv[...] = 1.0 / jnp.maximum(counts, 1.0)
    data_refs = list(blocks) if own_first else list(blocks) + [own]

    def step(q, carry):
        for g, ref in enumerate(data_refs):
            rows = pl.ds(g * chans, chans)
            for part in range(parts):
                got = opened(ref, q, part)
                scale = factor[rows, pl.ds(part * 128, 128)]
                limit = cap[rows, pl.ds(part * 128, 128)]
                lo = pl.ds(part * 128, 128)
                hi = pl.ds(half + part * 128, 128)
                for b in range(PACK):
                    real_part, imag_part = got[b], got[PACK + b]
                    power = real_part * real_part + imag_part * imag_part
                    phase = jnp.minimum(lax.rsqrt(power), limit)
                    white_re = (real_part * scale).astype(jnp.bfloat16)
                    white_im = (imag_part * scale).astype(jnp.bfloat16)
                    unit_re = (real_part * phase).astype(jnp.bfloat16)
                    unit_im = (imag_part * phase).astype(jnp.bfloat16)
                    if g < groups:
                        src_white[b, rows, lo] = white_re
                        src_white[b, rows, hi] = white_im
                        src_unit[b, rows, lo] = unit_re
                        src_unit[b, rows, hi] = unit_im
                    if g == (0 if own_first else groups):
                        for t in range(4):
                            at = pl.ds(t * chans, chans)
                            recv_white[b, at, lo] = white_im if t % 2 else white_re
                            recv_white[b, at, hi] = -white_re if t % 2 else white_im
                        for t in range(8):
                            at = pl.ds(t * chans, chans)
                            odd = (t + t // 4) % 2
                            recv_unit[b, at, lo] = unit_im if odd else unit_re
                            recv_unit[b, at, hi] = -unit_re if odd else unit_im
        scaled = inv[...]
        lane = lax.broadcasted_iota(jnp.int32, scaled.shape, 1)
        for b in range(PACK):
            lin = lax.dot_general(
                src_white[b], recv_white[b], (((1,), (1,)), ((), ())), preferred_element_type=jnp.float32
            )
            pha = lax.dot_general(
                src_unit[b], recv_unit[b], (((1,), (1,)), ((), ())), preferred_element_type=jnp.float32
            )
            mean = lin * scaled
            one = pha[:, :128] * scaled
            two = pha[:, 128:] * scaled
            coher = one * one + two * two
            both = jnp.where(lane < 2 * chans, mean, mean * coher)
            for g in range(groups):
                for h in range(per_group):
                    at = g * chans + h * rows_out
                    out[pos_ref[g] * per_group + h, q * PACK + b] = both[at : at + rows_out]
        return carry

    lax.fori_loop(0, slots, step, 0)


def lag_kernel(pieces, tile, rows_out, windows, freq, *rest):
    refs, (table_high, table_low, linear, weighted) = rest[:pieces], rest[pieces:]
    chans = linear.shape[1]
    first = pl.program_id(0) * tile
    lin_rows, pw_rows = [], []
    factor = math.sqrt(windows / freq)
    for i in range(tile):
        got = []
        for ref in refs:
            got.append(ref[pl.ds(first + i, ref.shape[0] // rows_out, stride=rows_out), :])
        flipped = (jnp.concatenate(got, axis=0) if pieces > 1 else got[0]).T
        lin_rows.append(jnp.concatenate([flipped[:chans], flipped[chans : 2 * chans]], axis=1))
        pw_rows.append(jnp.concatenate([flipped[2 * chans : 3 * chans], flipped[3 * chans :]], axis=1))
    for rows, out, gain in ((lin_rows, linear, factor), (pw_rows, weighted, factor * windows)):
        value = jnp.concatenate(rows, axis=0) * gain
        high = value.astype(jnp.bfloat16)
        low = (value - high.astype(jnp.float32)).astype(jnp.bfloat16)
        total = jnp.dot(high, table_high[...], preferred_element_type=jnp.float32)
        total += jnp.dot(high, table_low[...], preferred_element_type=jnp.float32)
        total += jnp.dot(low, table_high[...], preferred_element_type=jnp.float32)
        out[...] = total.reshape(tile, chans, LAGS)


def lag_table(freq, devs, sizes):
    slots = freq // PACK // devs
    order = []
    start = 0
    for size in sizes:
        for d in range(devs):
            for q in range(start, start + size):
                for b in range(PACK):
                    order.append(b * (freq // PACK) + d * slots + q)
        start += size
    bins = lowest_bin + np.asarray(order, np.int64)
    shifts = np.arange(LAGS, dtype=np.int64) - LAGS // 2
    theta = np.mod(bins[:, None] * shifts[None, :], window_samples) * (2.0 * math.pi / window_samples)
    table = np.concatenate([np.cos(theta), -np.sin(theta)], axis=0).astype(np.float32)
    high = table.astype(ml_dtypes.bfloat16)
    low = (table - high.astype(np.float32)).astype(ml_dtypes.bfloat16)
    return high, low


def body(spectra, valid, source_block):
    kinds, win_dev, chans, freq = spectra.shape
    devs = lax.axis_size("win")
    stations = lax.axis_size("chan")
    groups = source_block.shape[0]
    slots = freq // PACK // devs
    sizes = chunk_sizes(slots)
    rows_out = SRC_W // devs
    windows = win_dev * devs
    own_first = stations == groups
    params = pltpu.CompilerParams(vmem_limit_bytes=VMEM)

    mask = jnp.tile(valid.astype(jnp.float32).T, (1, 128 // win_dev))
    packed = pl.pallas_call(
        functools.partial(pack_kernel, sizes, devs),
        out_shape=[
            jax.ShapeDtypeStruct((devs, n + (i == 0), chans, 128), jnp.bfloat16) for i, n in enumerate(sizes)
        ],
        scratch_shapes=[
            pltpu.VMEM((freq // 128, kinds * win_dev * chans, 128), jnp.float32),
            pltpu.VMEM((freq // PACK * chans, 128), jnp.float32),
        ],
        compiler_params=params,
        name="pack",
    )(spectra, mask)

    me = lax.axis_index("chan")
    if own_first:
        held = lax.rem(me - jnp.arange(groups, dtype=jnp.int32) + stations, stations)
        pos = jnp.argmax(source_block[None, :] == held[:, None], axis=1).astype(jnp.int32)
    else:
        pos = jnp.arange(groups, dtype=jnp.int32)

    ring = [(i, (i + 1) % stations) for i in range(stations)]
    scale_blocks = None
    pieces = []
    for i, n in enumerate(sizes):
        mine = lax.all_to_all(packed[i], "win", 0, 0, tiled=True)
        if own_first:
            got = [mine]
            for hop in range(groups - 1):
                got.append(lax.ppermute(got[-1], "chan", ring))
        else:
            every = lax.all_gather(mine, "chan")
            got = [lax.dynamic_index_in_dim(every, source_block[g], 0, False) for g in range(groups)]
            got.append(mine)
        if i == 0:
            scale_blocks = got
        rows = groups * chans if own_first else (groups + 1) * chans
        half = win_dev * devs
        last = sizes[0]
        whole = pl.BlockSpec((devs, n + (i == 0), chans, 128), lambda s: (0, 0, 0, 0))
        tail = pl.BlockSpec((devs, 1, chans, 128), lambda s: (0, last, 0, 0))
        out = pl.pallas_call(
            functools.partial(cross_kernel, groups, own_first),
            grid=(1,),
            in_specs=[pl.BlockSpec(memory_space=pltpu.SMEM)] + [whole] * len(got) + [tail] * len(got),
            out_specs=pl.BlockSpec((devs, n * PACK, rows_out, 128), lambda s: (0, 0, 0, 0)),
            out_shape=jax.ShapeDtypeStruct((devs, n * PACK, rows_out, 128), jnp.float32),
            scratch_shapes=[
                pltpu.VMEM((rows, half), jnp.float32),
                pltpu.VMEM((rows, half), jnp.float32),
                pltpu.VMEM((PACK, groups * chans, 2 * half), jnp.bfloat16),
                pltpu.VMEM((PACK, groups * chans, 2 * half), jnp.bfloat16),
                pltpu.VMEM((PACK, 4 * chans, 2 * half), jnp.bfloat16),
                pltpu.VMEM((PACK, 8 * chans, 2 * half), jnp.bfloat16),
                pltpu.VMEM((groups * chans, 128), jnp.float32),
            ],
            compiler_params=params,
            name="cross",
        )(pos, *got, *scale_blocks)
        back = lax.all_to_all(out, "win", 0, 0, tiled=True)
        pieces.append(back.reshape(devs * n * PACK * rows_out, 128))

    high, low = lag_table(freq, devs, sizes)
    tile = 4
    full = lambda shape: pl.BlockSpec(shape, lambda s: (0, 0))
    return pl.pallas_call(
        functools.partial(lag_kernel, len(pieces), tile, rows_out, windows, freq),
        grid=(rows_out // tile,),
        in_specs=[full(p.shape) for p in pieces] + [full(high.shape), full(low.shape)],
        out_specs=[pl.BlockSpec((tile, chans, LAGS), lambda s: (s, 0, 0))] * 2,
        out_shape=[jax.ShapeDtypeStruct((rows_out, chans, LAGS), jnp.float32)] * 2,
        compiler_params=params,
        name="lag",
    )(*pieces, jnp.asarray(high), jnp.asarray(low))


def solution(mesh):
    placed = (P(None, "win", "chan", None), P("win", "chan"), P())
    return jax.shard_map(
        body,
        mesh=mesh,
        in_specs=placed,
        out_specs=(P("win", "chan", None), P("win", "chan", None)),
        check_vma=False,
    )
```

```python
import functools
import math

import jax
import jax.numpy as jnp
import ml_dtypes
import numpy as np
from jax import lax
from jax.experimental import pallas as pl
from jax.experimental.pallas import tpu as pltpu
from jax.sharding import PartitionSpec as P

LAGS = 1024
SRC_W = 128

lowest_bin = 60
window_samples = 15000
amp_eps = 1e-05
phase_floor = 0.5

ROWS = 3
PACK = 4
CHUNKS = (1 / 2, 1 / 2)
W_IN = 1
W_Z = 1
W_X = 1
W_O = 0
VMEM = 60 * 1024 * 1024


def cost(micros):
    return pl.CostEstimate(flops=0, bytes_accessed=int(micros * 3.0e6), transcendentals=0)


def chunk_sizes(slots):
    edges = [0]
    total = 0.0
    for share in CHUNKS:
        total += share
        edges.append(round(slots * total))
    return [edges[i + 1] - edges[i] for i in range(len(CHUNKS))]


def pack_kernel(sizes, devs, spectra_ref, valid_ref, *rest):
    outs, (wide, turned) = rest[: len(sizes)], rest[len(sizes) :]
    kinds, windows, chans, freq = spectra_ref.shape
    span = freq // PACK
    slots = span // devs
    real_part = spectra_ref[0].astype(jnp.float32)
    imag_part = spectra_ref[1].astype(jnp.float32)
    for i in range(freq // 128):
        cut = slice(i * 128, (i + 1) * 128)
        wide[i, pl.ds(0, windows * chans), :] = real_part[:, :, cut].reshape(windows * chans, 128)
        wide[i, pl.ds(windows * chans, windows * chans), :] = imag_part[:, :, cut].reshape(windows * chans, 128)
    total = jnp.sum(real_part * real_part + imag_part * imag_part, axis=-1, keepdims=True)
    mask = jnp.concatenate([valid_ref[...].astype(jnp.float32)] * (128 // windows), axis=0).T
    lane = lax.broadcasted_iota(jnp.int32, (chans, 128), 1)
    energy = jnp.zeros((chans, 128), jnp.float32)
    for w in range(windows):
        energy = jnp.where(lane % windows == w, total[w], energy)
    scale = mask / jnp.sqrt(energy * (1.0 / freq) + amp_eps)
    high = scale.astype(jnp.bfloat16).astype(jnp.float32)
    middle = (scale - high).astype(jnp.bfloat16).astype(jnp.float32)
    low = scale - high - middle
    part = lane // windows
    split = jnp.where(part == 0, high, jnp.where(part == 1, middle, jnp.where(part == 2, low, 0.0)))
    for c in range(chans):
        rows = []
        for k in range(kinds):
            rows_at = pl.ds(k * windows * chans + c, windows, stride=chans)
            line = jnp.concatenate([wide[i, rows_at, :] for i in range(freq // 128)], axis=1)
            for b in range(PACK):
                moved = line if b == 0 else pltpu.roll(line, freq - b * span, 1)
                rows.append(moved[:, :128])
        flipped = jnp.concatenate(rows, axis=0).T
        turned[pl.ds(c, span, stride=chans), :] = flipped[:span]
    for d in range(devs):
        start = d * slots
        for i, out in enumerate(outs):
            block = turned[pl.ds(start * chans, sizes[i] * chans), :]
            out[d, : sizes[i]] = block.astype(jnp.bfloat16).reshape(sizes[i], chans, 128)
            if i == 0:
                out[d, sizes[0]] = split.astype(jnp.bfloat16)
            start += sizes[i]


def swap_blocks(arrays, width):
    arrays = list(arrays)
    lane = lax.broadcasted_iota(jnp.int32, arrays[0].shape, 1)
    bit = 1
    while bit < len(arrays):
        upper = (lane // (width * bit)) % 2 == 1
        for i in range(len(arrays)):
            if i & bit == 0:
                a, c = arrays[i], arrays[i | bit]
                arrays[i] = jnp.where(upper, pltpu.roll(c, width * bit, 1), a)
                arrays[i | bit] = jnp.where(upper, c, pltpu.roll(a, 128 - width * bit, 1))
        bit *= 2
    return arrays


def cross_kernel(groups, own_first, rows_ref, *rest):
    blocks = rest[:groups]
    rest = rest[groups:]
    own = blocks[0]
    if not own_first:
        own, rest = rest[0], rest[1:]
    scales = rest[:groups]
    rest = rest[groups:]
    own_scale = scales[0]
    if not own_first:
        own_scale, rest = rest[0], rest[1:]
    devs, chans = own_scale.shape[0], own_scale.shape[2]
    outs, rest = rest[:devs], rest[devs:]
    factor, cap, src_white, src_unit, recv_white, recv_unit, inv, packed = rest
    width = 128 // 8
    parts = devs // 8
    half = parts * 128
    slots = outs[0].shape[0] // ROWS
    rows_out = outs[0].shape[1]

    def opened(ref, q, part):
        return swap_blocks([ref[part * 8 + d, q].astype(jnp.float32) for d in range(8)], width)

    scale_refs = list(scales) if own_first else list(scales) + [own_scale]
    for g, ref in enumerate(scale_refs):
        for part in range(parts):
            got = opened(ref, 0, part)
            value = got[0] + got[1] + got[2]
            factor[pl.ds(g * chans, chans), pl.ds(part * 128, 128)] = value
            cap[pl.ds(g * chans, chans), pl.ds(part * 128, 128)] = jnp.where(value > 0, 1.0 / phase_floor, 0.0)
    masks = jnp.where(cap[...] > 0, 1.0, 0.0).astype(jnp.bfloat16)
    mine = 0 if own_first else groups * chans
    recv = jnp.concatenate([masks[mine : mine + chans]] * 4, axis=0)
    counts = lax.dot_general(
        masks[: groups * chans], recv, (((1,), (1,)), ((), ())), preferred_element_type=jnp.float32
    )
    inv[...] = 1.0 / jnp.maximum(counts, 1.0)
    data_refs = list(blocks) if own_first else list(blocks) + [own]

    def step(q, carry):
        for g, ref in enumerate(data_refs):
            rows = pl.ds(g * chans, chans)
            for part in range(parts):
                got = opened(ref, q, part)
                scale = factor[rows, pl.ds(part * 128, 128)]
                limit = cap[rows, pl.ds(part * 128, 128)]
                lo = pl.ds(part * 128, 128)
                hi = pl.ds(half + part * 128, 128)
                for b in range(PACK):
                    real_part, imag_part = got[b], got[PACK + b]
                    power = real_part * real_part + imag_part * imag_part
                    phase = jnp.minimum(lax.rsqrt(power), limit)
                    white_re = (real_part * scale).astype(jnp.bfloat16)
                    white_im = (imag_part * scale).astype(jnp.bfloat16)
                    unit_re = (real_part * phase).astype(jnp.bfloat16)
                    unit_im = (imag_part * phase).astype(jnp.bfloat16)
                    if g < groups:
                        src_white[b, rows, lo] = white_re
                        src_white[b, rows, hi] = white_im
                        src_unit[b, rows, lo] = unit_re
                        src_unit[b, rows, hi] = unit_im
                    if g == (0 if own_first else groups):
                        for t in range(4):
                            at = pl.ds(t * chans, chans)
                            recv_white[b, at, lo] = white_im if t % 2 else white_re
                            recv_white[b, at, hi] = -white_re if t % 2 else white_im
                        for t in range(8):
                            at = pl.ds(t * chans, chans)
                            odd = (t + t // 4) % 2
                            recv_unit[b, at, lo] = unit_im if odd else unit_re
                            recv_unit[b, at, hi] = -unit_re if odd else unit_im
        scaled = inv[...]
        lane = lax.broadcasted_iota(jnp.int32, scaled.shape, 1)
        means, cohers = [], []
        for b in range(PACK):
            lin = lax.dot_general(
                src_white[b], recv_white[b], (((1,), (1,)), ((), ())), preferred_element_type=jnp.float32
            )
            pha = lax.dot_general(
                src_unit[b], recv_unit[b], (((1,), (1,)), ((), ())), preferred_element_type=jnp.float32
            )
            means.append(lin * scaled)
            one = pha[:, :128] * scaled
            two = pha[:, 128:] * scaled
            cohers.append(one * one + two * two)
        packed[0] = jnp.where(lane < 2 * chans, means[0], means[1])
        packed[1] = jnp.where(lane < 2 * chans, means[2], means[3])
        low = jnp.where(lane < chans, cohers[0], cohers[1])
        high = jnp.where(lane < 3 * chans, cohers[2], cohers[3])
        packed[2] = jnp.where(lane < 2 * chans, low, high)
        for m, out in enumerate(outs):
            at = pl.ds(pl.multiple_of(rows_ref[m], rows_out), rows_out)
            for t in range(ROWS):
                out[q * ROWS + t] = packed[t, at, :]
        return carry

    lax.fori_loop(0, slots, step, 0, unroll=2)


def lag_kernel(slots, devs, rows_out, windows, freq, pieces, first, me_ref, *rest):
    refs, rest = rest[:pieces], rest[pieces:]
    table_high, table_low, rest = rest[0], rest[1], rest[2:]
    if not first:
        linear_before, weighted_before, rest = rest[0], rest[1], rest[2:]
    linear, weighted, staged, left_high, left_low = rest
    chans = linear.shape[1]
    side = 128 // 2
    room = side // devs
    factor = math.sqrt(windows / freq)

    @pl.when(pl.program_id(0) == 0)
    def fill():
        def store(rows, value):
            high = value.astype(jnp.bfloat16)
            left_high[rows, :] = high
            left_low[rows, :] = (value - high.astype(jnp.float32)).astype(jnp.bfloat16)

        pad = jnp.zeros((max(room - slots, 1), 128), jnp.float32)
        lane = lax.broadcasted_iota(jnp.int32, (chans, 128), 1)
        for s in range(rows_out):
            for m in range(devs):
                at = pl.multiple_of((me_ref[0] ^ m) * room, room)
                for t, places in enumerate(((0,), (1,), (2, 3))):
                    block = refs[m][pl.ds(t * rows_out + s, slots, stride=ROWS * rows_out), :]
                    block = jnp.concatenate([block, pad], axis=0) if room > slots else block
                    for place in places:
                        staged[pl.ds(place * side + at, room), :] = block
            means = staged[: 2 * side].T * factor
            coher = staged[2 * side :].T * windows
            blocks = [coher[b * chans : (b + 1) * chans] for b in range(PACK)]
            weights = [jnp.where(lane < side, blocks[0], blocks[2]), jnp.where(lane < side, blocks[1], blocks[3])]
            parts = [means[i * chans : (i + 1) * chans] for i in range(4)]
            plain = [parts[0], parts[2], parts[1], parts[3]]
            store(pl.ds(s * chans, chans), jnp.concatenate(plain, axis=1))
            scaled = [part * weights[i % 2] for i, part in enumerate(plain)]
            store(pl.ds((rows_out + s) * chans, chans), jnp.concatenate(scaled, axis=1))

    total = jnp.dot(left_high[...], table_high[...], preferred_element_type=jnp.float32)
    total += jnp.dot(left_high[...], table_low[...], preferred_element_type=jnp.float32)
    total += jnp.dot(left_low[...], table_high[...], preferred_element_type=jnp.float32)
    half = rows_out * chans
    for out, share, before in (
        (linear, total[:half], None if first else linear_before),
        (weighted, total[half:], None if first else weighted_before),
    ):
        share = share.reshape(out.shape)
        out[...] = share if first else share + before[...]


def lag_table(freq, devs, start, count):
    span = freq // PACK
    slots = span // devs
    room = 128 // 2 // devs
    shifts = np.arange(LAGS, dtype=np.int64) - LAGS // 2
    bins = lowest_bin + np.arange(freq, dtype=np.int64)
    theta = np.mod(bins[:, None] * shifts[None, :], window_samples) * (2.0 * math.pi / window_samples)
    table = np.zeros((2, 2, 2, devs, room, LAGS), np.float32)
    for kind, values in enumerate((np.cos(theta), -np.sin(theta))):
        values = values.reshape(PACK, devs, slots, LAGS)[:, :, start : start + count]
        for b in range(PACK):
            table[kind, b % 2, b // 2, :, :count] = values[b]
    table = table.reshape(-1, LAGS)
    high = table.astype(ml_dtypes.bfloat16)
    low = (table - high.astype(np.float32)).astype(ml_dtypes.bfloat16)
    return high, low


def join_kernel(*refs):
    pass


def join(token, arrays):
    anywhere = pl.BlockSpec(memory_space=pl.ANY)
    return pl.pallas_call(
        join_kernel,
        in_specs=[anywhere] * (1 + len(arrays)),
        out_specs=anywhere,
        out_shape=jax.ShapeDtypeStruct(token.shape, token.dtype),
        input_output_aliases={0: 0},
        cost_estimate=cost(0.1),
        name="join",
    )(token, *arrays)


def body(spectra, valid, source_block):
    kinds, win_dev, chans, freq = spectra.shape
    devs = lax.axis_size("win")
    stations = lax.axis_size("chan")
    groups = source_block.shape[0]
    slots = freq // PACK // devs
    sizes = chunk_sizes(slots)
    rows_out = SRC_W // devs
    windows = win_dev * devs
    own_first = stations == groups == 4
    params = pltpu.CompilerParams(vmem_limit_bytes=VMEM)

    packed = pl.pallas_call(
        functools.partial(pack_kernel, sizes, devs),
        out_shape=[
            jax.ShapeDtypeStruct((devs, n + (i == 0), chans, 128), jnp.bfloat16) for i, n in enumerate(sizes)
        ],
        scratch_shapes=[
            pltpu.VMEM((freq // 128, kinds * win_dev * chans, 128), jnp.float32),
            pltpu.VMEM((freq // PACK * chans, 128), jnp.float32),
        ],
        compiler_params=params,
        cost_estimate=cost(5),
        name="pack",
    )(spectra, valid)

    me = lax.axis_index("chan")
    if own_first:
        held = lax.rem(me - jnp.arange(groups, dtype=jnp.int32) + stations, stations)
        pos = jnp.argmax(source_block[None, :] == held[:, None], axis=1).astype(jnp.int32)
    else:
        pos = jnp.arange(groups, dtype=jnp.int32)

    me_win = lax.axis_index("win")
    per_group = chans // rows_out
    target = me_win ^ jnp.arange(devs, dtype=jnp.int32)
    holder = jnp.argmax(pos[None, :] == (target // per_group)[:, None], axis=1).astype(jnp.int32)
    row_table = holder * chans + target % per_group * rows_out

    ring = [(i, (i + 1) % stations) for i in range(stations)]
    count = len(sizes)

    def cross_call(i, token, got, heads):
        n = sizes[i]
        rows = groups * chans if own_first else (groups + 1) * chans
        half = win_dev * devs
        last = sizes[0]
        whole = pl.BlockSpec((devs, n + (i == 0), chans, 128), lambda s: (0, 0, 0, 0))
        tail = pl.BlockSpec((devs, 1, chans, 128), lambda s: (0, last, 0, 0))
        shape = (n * ROWS, rows_out, 128)
        return pl.pallas_call(
            functools.partial(cross_kernel, groups, own_first),
            grid=(1,),
            in_specs=[pl.BlockSpec(memory_space=pltpu.SMEM)] + [whole] * len(got) + [tail] * len(got),
            out_specs=[pl.BlockSpec(shape, lambda s: (0, 0, 0))] * devs,
            out_shape=[jax.ShapeDtypeStruct(shape, jnp.float32)] * devs,
            scratch_shapes=[
                pltpu.VMEM((rows, half), jnp.float32),
                pltpu.VMEM((rows, half), jnp.float32),
                pltpu.VMEM((PACK, groups * chans, 2 * half), jnp.bfloat16),
                pltpu.VMEM((PACK, groups * chans, 2 * half), jnp.bfloat16),
                pltpu.VMEM((PACK, 4 * chans, 2 * half), jnp.bfloat16),
                pltpu.VMEM((PACK, 8 * chans, 2 * half), jnp.bfloat16),
                pltpu.VMEM((groups * chans, 128), jnp.float32),
                pltpu.VMEM((ROWS, groups * chans, 128), jnp.float32),
            ],
            compiler_params=params,
            cost_estimate=cost(2 + n),
            name="cross",
        )(token, *got, *heads)

    def send_back(outs):
        back = [outs[0]]
        for m in range(1, devs):
            back.append(lax.ppermute(outs[m], "win", [(d, d ^ m) for d in range(devs)]))
        return back

    backs = [None] * count
    if own_first:
        back_ring = [(i, (i - 1) % stations) for i in range(stations)]
        held = {}
        crossed = {}

        def enter(i, after):
            block = join(packed[i], after) if after else packed[i]
            held[i] = [lax.all_to_all(block, "win", 0, 0, tiled=True)]

        def spread(i, after):
            own = join(held[i][0], after) if after else held[i][0]
            up = lax.ppermute(own, "chan", ring)
            down = lax.ppermute(own, "chan", back_ring)
            held[i] = [own, up, lax.ppermute(up, "chan", ring), down]

        def cross_chunk(i, after):
            token = join(row_table, after) if after else row_table
            crossed[i] = cross_call(i, token, held[i], held[0])
            backs[i] = send_back(crossed[i])

        enter(0, [])
        for i in range(count + 1):
            if i < count:
                after = []
                if i and W_Z:
                    after.append(held[i - 1][1])
                if i > 1 and W_X:
                    after.append(crossed[i - 2][0])
                spread(i, after)
                if i + 1 < count:
                    enter(i + 1, [held[max(i - 1, 0)][0 if i == 0 else 1]] if W_IN else [])
            if i:
                cross_chunk(i - 1, [backs[i - 2][-1]] if W_O and i > 1 else [])
    else:
        gathered = []
        for p in packed:
            mine = lax.all_to_all(p, "win", 0, 0, tiled=True)
            every = lax.all_gather(mine, "chan")
            picked = [lax.dynamic_index_in_dim(every, source_block[g], 0, False) for g in range(groups)]
            gathered.append(picked + [mine])
        for i in range(count):
            backs[i] = send_back(cross_call(i, row_table, gathered[i], gathered[0]))

    tile = 256
    result = []
    whole_out = jax.ShapeDtypeStruct((rows_out, chans, LAGS), jnp.float32)
    out_spec = pl.BlockSpec((rows_out, chans, tile), lambda s: (0, 0, s))
    start = 0
    for i, n in enumerate(sizes):
        pieces = [back.reshape(-1, 128) for back in backs[i]]
        high, low = lag_table(freq, devs, start, n)
        table_spec = pl.BlockSpec((high.shape[0], tile), lambda s: (0, s))
        result = pl.pallas_call(
            functools.partial(lag_kernel, n, devs, rows_out, windows, freq, len(pieces), i == 0),
            grid=(LAGS // tile,),
            in_specs=[pl.BlockSpec(memory_space=pltpu.SMEM)] + [pl.BlockSpec(pieces[0].shape, lambda s: (0, 0))] * len(pieces)
            + [table_spec] * 2
            + [out_spec] * len(result),
            out_specs=[out_spec] * 2,
            out_shape=[whole_out] * 2,
            scratch_shapes=[
                pltpu.VMEM((2 * 128, 128), jnp.float32),
                pltpu.VMEM((2 * rows_out * chans, high.shape[0]), jnp.bfloat16),
                pltpu.VMEM((2 * rows_out * chans, high.shape[0]), jnp.bfloat16),
            ],
            compiler_params=params,
            cost_estimate=cost(6),
            name="lag",
        )(me_win.reshape(1), *pieces, jnp.asarray(high), jnp.asarray(low), *result)
        start += n
    return result


def solution(mesh):
    placed = (P(None, "win", "chan", None), P("win", "chan"), P())
    return jax.shard_map(
        body,
        mesh=mesh,
        in_specs=placed,
        out_specs=(P("win", "chan", None), P("win", "chan", None)),
        check_vma=False,
    )
```

```python
import functools
import math

import jax
import jax.numpy as jnp
import ml_dtypes
import numpy as np
from jax import lax
from jax.experimental import pallas as pl
from jax.experimental.pallas import tpu as pltpu
from jax.sharding import PartitionSpec as P

LAGS = 1024
SRC_W = 128

lowest_bin = 60
window_samples = 15000
amp_eps = 1e-05
phase_floor = 0.5

ROWS = 3
PACK = 4
CHUNKS = (1 / 2, 1 / 2)
W_IN = 1
W_Z = 1
W_X = 1
W_O = 0
VMEM = 60 * 1024 * 1024


def cost(micros):
    return pl.CostEstimate(flops=0, bytes_accessed=int(micros * 3.0e6), transcendentals=0)


def chunk_sizes(slots):
    edges = [0]
    total = 0.0
    for share in CHUNKS:
        total += share
        edges.append(round(slots * total))
    return [edges[i + 1] - edges[i] for i in range(len(CHUNKS))]


def pack_kernel(sizes, devs, spectra_ref, valid_ref, *rest):
    outs, (wide, turned) = rest[: len(sizes)], rest[len(sizes) :]
    kinds, windows, chans, freq = spectra_ref.shape
    span = freq // PACK
    slots = span // devs
    real_part = spectra_ref[0].astype(jnp.float32)
    imag_part = spectra_ref[1].astype(jnp.float32)
    for i in range(freq // 128):
        cut = slice(i * 128, (i + 1) * 128)
        wide[i, pl.ds(0, windows * chans), :] = real_part[:, :, cut].reshape(windows * chans, 128)
        wide[i, pl.ds(windows * chans, windows * chans), :] = imag_part[:, :, cut].reshape(windows * chans, 128)
    total = jnp.sum(real_part * real_part + imag_part * imag_part, axis=-1, keepdims=True)
    mask = jnp.concatenate([valid_ref[...].astype(jnp.float32)] * (128 // windows), axis=0).T
    lane = lax.broadcasted_iota(jnp.int32, (chans, 128), 1)
    energy = jnp.zeros((chans, 128), jnp.float32)
    for w in range(windows):
        energy = jnp.where(lane % windows == w, total[w], energy)
    scale = mask / jnp.sqrt(energy * (1.0 / freq) + amp_eps)
    high = scale.astype(jnp.bfloat16).astype(jnp.float32)
    middle = (scale - high).astype(jnp.bfloat16).astype(jnp.float32)
    low = scale - high - middle
    part = lane // windows
    split = jnp.where(part == 0, high, jnp.where(part == 1, middle, jnp.where(part == 2, low, 0.0)))
    for c in range(chans):
        rows = []
        for k in range(kinds):
            rows_at = pl.ds(k * windows * chans + c, windows, stride=chans)
            line = jnp.concatenate([wide[i, rows_at, :] for i in range(freq // 128)], axis=1)
            for b in range(PACK):
                moved = line if b == 0 else pltpu.roll(line, freq - b * span, 1)
                rows.append(moved[:, :128])
        flipped = jnp.concatenate(rows, axis=0).T
        turned[pl.ds(c, span, stride=chans), :] = flipped[:span]
    for d in range(devs):
        start = d * slots
        for i, out in enumerate(outs):
            block = turned[pl.ds(start * chans, sizes[i] * chans), :]
            out[d, : sizes[i]] = block.astype(jnp.bfloat16).reshape(sizes[i], chans, 128)
            if i == 0:
                out[d, sizes[0]] = split.astype(jnp.bfloat16)
            start += sizes[i]


def swap_blocks(arrays, width):
    arrays = list(arrays)
    lane = lax.broadcasted_iota(jnp.int32, arrays[0].shape, 1)
    bit = 1
    while bit < len(arrays):
        upper = (lane // (width * bit)) % 2 == 1
        for i in range(len(arrays)):
            if i & bit == 0:
                a, c = arrays[i], arrays[i | bit]
                arrays[i] = jnp.where(upper, pltpu.roll(c, width * bit, 1), a)
                arrays[i | bit] = jnp.where(upper, c, pltpu.roll(a, 128 - width * bit, 1))
        bit *= 2
    return arrays


def cross_kernel(groups, own_first, rows_ref, *rest):
    blocks = rest[:groups]
    rest = rest[groups:]
    own = blocks[0]
    if not own_first:
        own, rest = rest[0], rest[1:]
    scales = rest[:groups]
    rest = rest[groups:]
    own_scale = scales[0]
    if not own_first:
        own_scale, rest = rest[0], rest[1:]
    devs, chans = own_scale.shape[0], own_scale.shape[2]
    outs, rest = rest[:devs], rest[devs:]
    factor, cap, src_white, src_unit, recv_white, recv_unit, inv, packed = rest
    width = 128 // 8
    parts = devs // 8
    half = parts * 128
    slots = outs[0].shape[0] // ROWS
    rows_out = outs[0].shape[1]

    def opened(ref, q, part):
        return swap_blocks([ref[part * 8 + d, q].astype(jnp.float32) for d in range(8)], width)

    scale_refs = list(scales) if own_first else list(scales) + [own_scale]
    for g, ref in enumerate(scale_refs):
        for part in range(parts):
            got = opened(ref, 0, part)
            value = got[0] + got[1] + got[2]
            factor[pl.ds(g * chans, chans), pl.ds(part * 128, 128)] = value
            cap[pl.ds(g * chans, chans), pl.ds(part * 128, 128)] = jnp.where(value > 0, 1.0 / phase_floor, 0.0)
    masks = jnp.where(cap[...] > 0, 1.0, 0.0).astype(jnp.bfloat16)
    mine = 0 if own_first else groups * chans
    recv = jnp.concatenate([masks[mine : mine + chans]] * 4, axis=0)
    counts = lax.dot_general(
        masks[: groups * chans], recv, (((1,), (1,)), ((), ())), preferred_element_type=jnp.float32
    )
    inv[...] = 1.0 / jnp.maximum(counts, 1.0)
    data_refs = list(blocks) if own_first else list(blocks) + [own]

    def step(q, carry):
        for g, ref in enumerate(data_refs):
            rows = pl.ds(g * chans, chans)
            for part in range(parts):
                got = opened(ref, q, part)
                scale = factor[rows, pl.ds(part * 128, 128)]
                limit = cap[rows, pl.ds(part * 128, 128)]
                lo = pl.ds(part * 128, 128)
                hi = pl.ds(half + part * 128, 128)
                for b in range(PACK):
                    real_part, imag_part = got[b], got[PACK + b]
                    power = real_part * real_part + imag_part * imag_part
                    phase = jnp.minimum(lax.rsqrt(power), limit)
                    white_re = (real_part * scale).astype(jnp.bfloat16)
                    white_im = (imag_part * scale).astype(jnp.bfloat16)
                    unit_re = (real_part * phase).astype(jnp.bfloat16)
                    unit_im = (imag_part * phase).astype(jnp.bfloat16)
                    if g < groups:
                        src_white[b, rows, lo] = white_re
                        src_white[b, rows, hi] = white_im
                        src_unit[b, rows, lo] = unit_re
                        src_unit[b, rows, hi] = unit_im
                    if g == (0 if own_first else groups):
                        for t in range(4):
                            at = pl.ds(t * chans, chans)
                            recv_white[b, at, lo] = white_im if t % 2 else white_re
                            recv_white[b, at, hi] = -white_re if t % 2 else white_im
                        for t in range(8):
                            at = pl.ds(t * chans, chans)
                            odd = (t + t // 4) % 2
                            recv_unit[b, at, lo] = unit_im if odd else unit_re
                            recv_unit[b, at, hi] = -unit_re if odd else unit_im
        scaled = inv[...]
        lane = lax.broadcasted_iota(jnp.int32, scaled.shape, 1)
        means, cohers = [], []
        for b in range(PACK):
            lin = lax.dot_general(
                src_white[b], recv_white[b], (((1,), (1,)), ((), ())), preferred_element_type=jnp.float32
            )
            pha = lax.dot_general(
                src_unit[b], recv_unit[b], (((1,), (1,)), ((), ())), preferred_element_type=jnp.float32
            )
            means.append(lin * scaled)
            one = pha[:, :128] * scaled
            two = pha[:, 128:] * scaled
            cohers.append(one * one + two * two)
        packed[0] = jnp.where(lane < 2 * chans, means[0], means[1])
        packed[1] = jnp.where(lane < 2 * chans, means[2], means[3])
        low = jnp.where(lane < chans, cohers[0], cohers[1])
        high = jnp.where(lane < 3 * chans, cohers[2], cohers[3])
        packed[2] = jnp.where(lane < 2 * chans, low, high)
        for m, out in enumerate(outs):
            at = pl.ds(pl.multiple_of(rows_ref[m], rows_out), rows_out)
            for t in range(ROWS):
                out[q * ROWS + t] = packed[t, at, :]
        return carry

    lax.fori_loop(0, slots, step, 0, unroll=2)


def lag_kernel(slots, devs, rows_out, windows, freq, pieces, first, me_ref, *rest):
    refs, rest = rest[:pieces], rest[pieces:]
    table_high, table_low, rest = rest[0], rest[1], rest[2:]
    if not first:
        linear_before, weighted_before, rest = rest[0], rest[1], rest[2:]
    linear, weighted, staged, left_high, left_low = rest
    chans = linear.shape[1]
    side = 128 // 2
    room = side // devs
    factor = math.sqrt(windows / freq)

    @pl.when(pl.program_id(0) == 0)
    def fill():
        def store(rows, value):
            high = value.astype(jnp.bfloat16)
            left_high[rows, :] = high
            left_low[rows, :] = (value - high.astype(jnp.float32)).astype(jnp.bfloat16)

        pad = jnp.zeros((max(room - slots, 1), 128), jnp.float32)
        lane = lax.broadcasted_iota(jnp.int32, (chans, 128), 1)
        for s in range(rows_out):
            for m in range(devs):
                at = pl.multiple_of((me_ref[0] ^ m) * room, room)
                for t, places in enumerate(((0,), (1,), (2, 3))):
                    block = refs[m][pl.ds(t * rows_out + s, slots, stride=ROWS * rows_out), :]
                    block = jnp.concatenate([block, pad], axis=0) if room > slots else block
                    for place in places:
                        staged[pl.ds(place * side + at, room), :] = block
            means = staged[: 2 * side].T * factor
            coher = staged[2 * side :].T * windows
            blocks = [coher[b * chans : (b + 1) * chans] for b in range(PACK)]
            weights = [jnp.where(lane < side, blocks[0], blocks[2]), jnp.where(lane < side, blocks[1], blocks[3])]
            parts = [means[i * chans : (i + 1) * chans] for i in range(4)]
            plain = [parts[0], parts[2], parts[1], parts[3]]
            store(pl.ds(s * chans, chans), jnp.concatenate(plain, axis=1))
            scaled = [part * weights[i % 2] for i, part in enumerate(plain)]
            store(pl.ds((rows_out + s) * chans, chans), jnp.concatenate(scaled, axis=1))

    total = jnp.dot(left_high[...], table_high[...], preferred_element_type=jnp.float32)
    total += jnp.dot(left_high[...], table_low[...], preferred_element_type=jnp.float32)
    total += jnp.dot(left_low[...], table_high[...], preferred_element_type=jnp.float32)
    half = rows_out * chans
    for out, share, before in (
        (linear, total[:half], None if first else linear_before),
        (weighted, total[half:], None if first else weighted_before),
    ):
        share = share.reshape(out.shape)
        out[...] = share if first else share + before[...]


def lag_table(freq, devs, start, count):
    span = freq // PACK
    slots = span // devs
    room = 128 // 2 // devs
    shifts = np.arange(LAGS, dtype=np.int64) - LAGS // 2
    bins = lowest_bin + np.arange(freq, dtype=np.int64)
    theta = np.mod(bins[:, None] * shifts[None, :], window_samples) * (2.0 * math.pi / window_samples)
    table = np.zeros((2, 2, 2, devs, room, LAGS), np.float32)
    for kind, values in enumerate((np.cos(theta), -np.sin(theta))):
        values = values.reshape(PACK, devs, slots, LAGS)[:, :, start : start + count]
        for b in range(PACK):
            table[kind, b % 2, b // 2, :, :count] = values[b]
    table = table.reshape(-1, LAGS)
    high = table.astype(ml_dtypes.bfloat16)
    low = (table - high.astype(np.float32)).astype(ml_dtypes.bfloat16)
    return high, low


def join_kernel(*refs):
    pass


def join(token, arrays):
    anywhere = pl.BlockSpec(memory_space=pl.ANY)
    return pl.pallas_call(
        join_kernel,
        in_specs=[anywhere] * (1 + len(arrays)),
        out_specs=anywhere,
        out_shape=jax.ShapeDtypeStruct(token.shape, token.dtype),
        input_output_aliases={0: 0},
        cost_estimate=cost(0.1),
        name="join",
    )(token, *arrays)


def body(spectra, valid, source_block):
    kinds, win_dev, chans, freq = spectra.shape
    devs = lax.axis_size("win")
    stations = lax.axis_size("chan")
    groups = source_block.shape[0]
    slots = freq // PACK // devs
    sizes = chunk_sizes(slots)
    rows_out = SRC_W // devs
    windows = win_dev * devs
    own_first = stations == groups == 4
    params = pltpu.CompilerParams(vmem_limit_bytes=VMEM)

    packed = pl.pallas_call(
        functools.partial(pack_kernel, sizes, devs),
        out_shape=[
            jax.ShapeDtypeStruct((devs, n + (i == 0), chans, 128), jnp.bfloat16) for i, n in enumerate(sizes)
        ],
        scratch_shapes=[
            pltpu.VMEM((freq // 128, kinds * win_dev * chans, 128), jnp.float32),
            pltpu.VMEM((freq // PACK * chans, 128), jnp.float32),
        ],
        compiler_params=params,
        cost_estimate=cost(5),
        name="pack",
    )(spectra, valid)

    me = lax.axis_index("chan")
    if own_first:
        held = lax.rem(me - jnp.arange(groups, dtype=jnp.int32) + stations, stations)
        pos = jnp.argmax(source_block[None, :] == held[:, None], axis=1).astype(jnp.int32)
    else:
        pos = jnp.arange(groups, dtype=jnp.int32)

    me_win = lax.axis_index("win")
    per_group = chans // rows_out
    target = me_win ^ jnp.arange(devs, dtype=jnp.int32)
    holder = jnp.argmax(pos[None, :] == (target // per_group)[:, None], axis=1).astype(jnp.int32)
    row_table = holder * chans + target % per_group * rows_out

    ring = [(i, (i + 1) % stations) for i in range(stations)]
    count = len(sizes)

    def cross_call(i, token, got, heads):
        n = sizes[i]
        rows = groups * chans if own_first else (groups + 1) * chans
        half = win_dev * devs
        last = sizes[0]
        whole = pl.BlockSpec((devs, n + (i == 0), chans, 128), lambda s: (0, 0, 0, 0))
        tail = pl.BlockSpec((devs, 1, chans, 128), lambda s: (0, last, 0, 0))
        shape = (n * ROWS, rows_out, 128)
        return pl.pallas_call(
            functools.partial(cross_kernel, groups, own_first),
            grid=(1,),
            in_specs=[pl.BlockSpec(memory_space=pltpu.SMEM)] + [whole] * len(got) + [tail] * len(got),
            out_specs=[pl.BlockSpec(shape, lambda s: (0, 0, 0))] * devs,
            out_shape=[jax.ShapeDtypeStruct(shape, jnp.float32)] * devs,
            scratch_shapes=[
                pltpu.VMEM((rows, half), jnp.float32),
                pltpu.VMEM((rows, half), jnp.float32),
                pltpu.VMEM((PACK, groups * chans, 2 * half), jnp.bfloat16),
                pltpu.VMEM((PACK, groups * chans, 2 * half), jnp.bfloat16),
                pltpu.VMEM((PACK, 4 * chans, 2 * half), jnp.bfloat16),
                pltpu.VMEM((PACK, 8 * chans, 2 * half), jnp.bfloat16),
                pltpu.VMEM((groups * chans, 128), jnp.float32),
                pltpu.VMEM((ROWS, groups * chans, 128), jnp.float32),
            ],
            compiler_params=params,
            cost_estimate=cost(2 + n),
            name="cross",
        )(token, *got, *heads)

    def send_back(outs):
        back = [outs[0]]
        for m in range(1, devs):
            back.append(lax.ppermute(outs[m], "win", [(d, d ^ m) for d in range(devs)]))
        return back

    backs = [None] * count
    if own_first:
        back_ring = [(i, (i - 1) % stations) for i in range(stations)]
        held = {}
        crossed = {}

        def enter(i, after):
            block = join(packed[i], after) if after else packed[i]
            held[i] = [lax.all_to_all(block, "win", 0, 0, tiled=True)]

        def spread(i, after):
            own = join(held[i][0], after) if after else held[i][0]
            up = lax.ppermute(own, "chan", ring)
            down = lax.ppermute(own, "chan", back_ring)
            held[i] = [own, up, lax.ppermute(up, "chan", ring), down]

        def cross_chunk(i, after):
            token = join(row_table, after) if after else row_table
            crossed[i] = cross_call(i, token, held[i], held[0])
            backs[i] = send_back(crossed[i])

        enter(0, [])
        for i in range(count + 1):
            if i < count:
                after = []
                if i and W_Z:
                    after.append(held[i - 1][3])
                if i > 1 and W_X:
                    after.append(crossed[i - 2][0])
                spread(i, after)
                if i + 1 < count:
                    enter(i + 1, [held[max(i - 1, 0)][0 if i == 0 else 1]] if W_IN else [])
            if i:
                cross_chunk(i - 1, [backs[i - 2][-1]] if W_O and i > 1 else [])
    else:
        gathered = []
        for p in packed:
            mine = lax.all_to_all(p, "win", 0, 0, tiled=True)
            every = lax.all_gather(mine, "chan")
            picked = [lax.dynamic_index_in_dim(every, source_block[g], 0, False) for g in range(groups)]
            gathered.append(picked + [mine])
        for i in range(count):
            backs[i] = send_back(cross_call(i, row_table, gathered[i], gathered[0]))

    tile = 256
    result = []
    whole_out = jax.ShapeDtypeStruct((rows_out, chans, LAGS), jnp.float32)
    out_spec = pl.BlockSpec((rows_out, chans, tile), lambda s: (0, 0, s))
    start = 0
    for i, n in enumerate(sizes):
        pieces = [back.reshape(-1, 128) for back in backs[i]]
        high, low = lag_table(freq, devs, start, n)
        table_spec = pl.BlockSpec((high.shape[0], tile), lambda s: (0, s))
        result = pl.pallas_call(
            functools.partial(lag_kernel, n, devs, rows_out, windows, freq, len(pieces), i == 0),
            grid=(LAGS // tile,),
            in_specs=[pl.BlockSpec(memory_space=pltpu.SMEM)] + [pl.BlockSpec(pieces[0].shape, lambda s: (0, 0))] * len(pieces)
            + [table_spec] * 2
            + [out_spec] * len(result),
            out_specs=[out_spec] * 2,
            out_shape=[whole_out] * 2,
            scratch_shapes=[
                pltpu.VMEM((2 * 128, 128), jnp.float32),
                pltpu.VMEM((2 * rows_out * chans, high.shape[0]), jnp.bfloat16),
                pltpu.VMEM((2 * rows_out * chans, high.shape[0]), jnp.bfloat16),
            ],
            compiler_params=params,
            cost_estimate=cost(6),
            name="lag",
        )(me_win.reshape(1), *pieces, jnp.asarray(high), jnp.asarray(low), *result)
        start += n
    return result


def solution(mesh):
    placed = (P(None, "win", "chan", None), P("win", "chan"), P())
    return jax.shard_map(
        body,
        mesh=mesh,
        in_specs=placed,
        out_specs=(P("win", "chan", None), P("win", "chan", None)),
        check_vma=False,
    )
```

```python
import functools
import math

import jax
import jax.numpy as jnp
import ml_dtypes
import numpy as np
from jax import lax
from jax.experimental import pallas as pl
from jax.experimental.pallas import tpu as pltpu
from jax.sharding import PartitionSpec as P

LAGS = 1024
SRC_W = 128

lowest_bin = 60
window_samples = 15000
amp_eps = 1e-05
phase_floor = 0.5

ROWS = 3
PACK = 4
CHUNKS = (1 / 2, 1 / 2)
W_IN = 0
W_Z = 1
W_X = 1
W_O = 0
VMEM = 24 * 1024 * 1024


def cost(micros):
    return pl.CostEstimate(flops=0, bytes_accessed=int(micros * 3.0e6), transcendentals=0)


def chunk_sizes(slots):
    edges = [0]
    total = 0.0
    for share in CHUNKS:
        total += share
        edges.append(round(slots * total))
    return [edges[i + 1] - edges[i] for i in range(len(CHUNKS))]


def pack_kernel(sizes, devs, spectra_ref, valid_ref, *rest):
    outs, (wide, turned) = rest[: len(sizes)], rest[len(sizes) :]
    kinds, windows, chans, freq = spectra_ref.shape
    span = freq // PACK
    slots = span // devs
    real_part = spectra_ref[0].astype(jnp.float32)
    imag_part = spectra_ref[1].astype(jnp.float32)
    for i in range(freq // 128):
        cut = slice(i * 128, (i + 1) * 128)
        wide[i, pl.ds(0, windows * chans), :] = real_part[:, :, cut].reshape(windows * chans, 128)
        wide[i, pl.ds(windows * chans, windows * chans), :] = imag_part[:, :, cut].reshape(windows * chans, 128)
    total = jnp.sum(real_part * real_part + imag_part * imag_part, axis=-1, keepdims=True)
    mask = jnp.concatenate([valid_ref[...].astype(jnp.float32)] * (128 // windows), axis=0).T
    lane = lax.broadcasted_iota(jnp.int32, (chans, 128), 1)
    energy = jnp.zeros((chans, 128), jnp.float32)
    for w in range(windows):
        energy = jnp.where(lane % windows == w, total[w], energy)
    scale = mask / jnp.sqrt(energy * (1.0 / freq) + amp_eps)
    high = scale.astype(jnp.bfloat16).astype(jnp.float32)
    middle = (scale - high).astype(jnp.bfloat16).astype(jnp.float32)
    low = scale - high - middle
    part = lane // windows
    split = jnp.where(part == 0, high, jnp.where(part == 1, middle, jnp.where(part == 2, low, 0.0)))
    for c in range(chans):
        rows = []
        for k in range(kinds):
            rows_at = pl.ds(k * windows * chans + c, windows, stride=chans)
            line = jnp.concatenate([wide[i, rows_at, :] for i in range(freq // 128)], axis=1)
            for b in range(PACK):
                moved = line if b == 0 else pltpu.roll(line, freq - b * span, 1)
                rows.append(moved[:, :128])
        flipped = jnp.concatenate(rows, axis=0).T
        turned[pl.ds(c, span, stride=chans), :] = flipped[:span]
    for d in range(devs):
        start = d * slots
        for i, out in enumerate(outs):
            block = turned[pl.ds(start * chans, sizes[i] * chans), :]
            out[d, : sizes[i]] = block.astype(jnp.bfloat16).reshape(sizes[i], chans, 128)
            if i == 0:
                out[d, sizes[0]] = split.astype(jnp.bfloat16)
            start += sizes[i]


def swap_blocks(arrays, width):
    arrays = list(arrays)
    lane = lax.broadcasted_iota(jnp.int32, arrays[0].shape, 1)
    bit = 1
    while bit < len(arrays):
        upper = (lane // (width * bit)) % 2 == 1
        for i in range(len(arrays)):
            if i & bit == 0:
                a, c = arrays[i], arrays[i | bit]
                arrays[i] = jnp.where(upper, pltpu.roll(c, width * bit, 1), a)
                arrays[i | bit] = jnp.where(upper, c, pltpu.roll(a, 128 - width * bit, 1))
        bit *= 2
    return arrays


def cross_kernel(groups, own_first, rows_ref, *rest):
    blocks = rest[:groups]
    rest = rest[groups:]
    own = blocks[0]
    if not own_first:
        own, rest = rest[0], rest[1:]
    scales = rest[:groups]
    rest = rest[groups:]
    own_scale = scales[0]
    if not own_first:
        own_scale, rest = rest[0], rest[1:]
    devs, chans = own_scale.shape[0], own_scale.shape[2]
    outs, rest = rest[:devs], rest[devs:]
    factor, cap, src_white, src_unit, recv_white, recv_unit, inv, packed = rest
    width = 128 // 8
    parts = devs // 8
    half = parts * 128
    slots = outs[0].shape[0] // ROWS
    rows_out = outs[0].shape[1]

    def opened(ref, q, part):
        moved = swap_blocks([ref[part * 8 + d, q] for d in range(8)], width)
        return [block.astype(jnp.float32) for block in moved]

    scale_refs = list(scales) if own_first else list(scales) + [own_scale]
    for g, ref in enumerate(scale_refs):
        for part in range(parts):
            got = opened(ref, 0, part)
            value = got[0] + got[1] + got[2]
            factor[pl.ds(g * chans, chans), pl.ds(part * 128, 128)] = value
            cap[pl.ds(g * chans, chans), pl.ds(part * 128, 128)] = jnp.where(value > 0, 1.0 / phase_floor, 0.0)
    masks = jnp.where(cap[...] > 0, 1.0, 0.0).astype(jnp.bfloat16)
    mine = 0 if own_first else groups * chans
    recv = jnp.concatenate([masks[mine : mine + chans]] * 4, axis=0)
    counts = lax.dot_general(
        masks[: groups * chans], recv, (((1,), (1,)), ((), ())), preferred_element_type=jnp.float32
    )
    inv[...] = 1.0 / jnp.maximum(counts, 1.0)
    data_refs = list(blocks) if own_first else list(blocks) + [own]

    def step(q, carry):
        for g, ref in enumerate(data_refs):
            rows = pl.ds(g * chans, chans)
            for part in range(parts):
                got = opened(ref, q, part)
                scale = factor[rows, pl.ds(part * 128, 128)]
                limit = cap[rows, pl.ds(part * 128, 128)]
                lo = pl.ds(part * 128, 128)
                hi = pl.ds(half + part * 128, 128)
                for b in range(PACK):
                    real_part, imag_part = got[b], got[PACK + b]
                    power = real_part * real_part + imag_part * imag_part
                    phase = jnp.minimum(lax.rsqrt(power), limit)
                    white_re = (real_part * scale).astype(jnp.bfloat16)
                    white_im = (imag_part * scale).astype(jnp.bfloat16)
                    unit_re = (real_part * phase).astype(jnp.bfloat16)
                    unit_im = (imag_part * phase).astype(jnp.bfloat16)
                    if g < groups:
                        src_white[b, rows, lo] = white_re
                        src_white[b, rows, hi] = white_im
                        src_unit[b, rows, lo] = unit_re
                        src_unit[b, rows, hi] = unit_im
                    if g == (0 if own_first else groups):
                        for t in range(4):
                            at = pl.ds(t * chans, chans)
                            recv_white[b, at, lo] = white_im if t % 2 else white_re
                            recv_white[b, at, hi] = -white_re if t % 2 else white_im
                        for t in range(8):
                            at = pl.ds(t * chans, chans)
                            odd = (t + t // 4) % 2
                            recv_unit[b, at, lo] = unit_im if odd else unit_re
                            recv_unit[b, at, hi] = -unit_re if odd else unit_im
        scaled = inv[...]
        lane = lax.broadcasted_iota(jnp.int32, scaled.shape, 1)
        means, cohers = [], []
        for b in range(PACK):
            lin = lax.dot_general(
                src_white[b], recv_white[b], (((1,), (1,)), ((), ())), preferred_element_type=jnp.float32
            )
            pha = lax.dot_general(
                src_unit[b], recv_unit[b], (((1,), (1,)), ((), ())), preferred_element_type=jnp.float32
            )
            means.append(lin * scaled)
            one = pha[:, :128] * scaled
            two = pha[:, 128:] * scaled
            cohers.append(one * one + two * two)
        packed[0] = jnp.where(lane < 2 * chans, means[0], means[1])
        packed[1] = jnp.where(lane < 2 * chans, means[2], means[3])
        low = jnp.where(lane < chans, cohers[0], cohers[1])
        high = jnp.where(lane < 3 * chans, cohers[2], cohers[3])
        packed[2] = jnp.where(lane < 2 * chans, low, high)
        for m, out in enumerate(outs):
            at = pl.ds(pl.multiple_of(rows_ref[m], rows_out), rows_out)
            for t in range(ROWS):
                out[q * ROWS + t] = packed[t, at, :]
        return carry

    lax.fori_loop(0, slots, step, 0, unroll=3)


def lag_kernel(slots, devs, rows_out, windows, freq, pieces, first, me_ref, *rest):
    refs, rest = rest[:pieces], rest[pieces:]
    table_high, table_low, rest = rest[0], rest[1], rest[2:]
    if not first:
        linear_before, weighted_before, rest = rest[0], rest[1], rest[2:]
    linear, weighted, staged, left_high, left_low = rest
    chans = linear.shape[1]
    side = 128 // 2
    room = side // devs
    factor = math.sqrt(windows / freq)

    @pl.when(pl.program_id(0) == 0)
    def fill():
        def store(rows, value):
            high = value.astype(jnp.bfloat16)
            left_high[rows, :] = high
            left_low[rows, :] = (value - high.astype(jnp.float32)).astype(jnp.bfloat16)

        pad = jnp.zeros((max(room - slots, 1), 128), jnp.float32)
        lane = lax.broadcasted_iota(jnp.int32, (chans, 128), 1)
        for s in range(rows_out):
            for m in range(devs):
                at = pl.multiple_of((me_ref[0] ^ m) * room, room)
                for t, places in enumerate(((0,), (1,), (2, 3))):
                    block = refs[m][pl.ds(t * rows_out + s, slots, stride=ROWS * rows_out), :]
                    block = jnp.concatenate([block, pad], axis=0) if room > slots else block
                    for place in places:
                        staged[pl.ds(place * side + at, room), :] = block
            means = staged[: 2 * side].T * factor
            coher = staged[2 * side :].T * windows
            blocks = [coher[b * chans : (b + 1) * chans] for b in range(PACK)]
            weights = [jnp.where(lane < side, blocks[0], blocks[2]), jnp.where(lane < side, blocks[1], blocks[3])]
            parts = [means[i * chans : (i + 1) * chans] for i in range(4)]
            plain = [parts[0], parts[2], parts[1], parts[3]]
            store(pl.ds(s * chans, chans), jnp.concatenate(plain, axis=1))
            scaled = [part * weights[i % 2] for i, part in enumerate(plain)]
            store(pl.ds((rows_out + s) * chans, chans), jnp.concatenate(scaled, axis=1))

    total = jnp.dot(left_high[...], table_high[...], preferred_element_type=jnp.float32)
    total += jnp.dot(left_high[...], table_low[...], preferred_element_type=jnp.float32)
    total += jnp.dot(left_low[...], table_high[...], preferred_element_type=jnp.float32)
    half = rows_out * chans
    for out, share, before in (
        (linear, total[:half], None if first else linear_before),
        (weighted, total[half:], None if first else weighted_before),
    ):
        share = share.reshape(out.shape)
        out[...] = share if first else share + before[...]


def lag_table(freq, devs, start, count):
    span = freq // PACK
    slots = span // devs
    room = 128 // 2 // devs
    shifts = np.arange(LAGS, dtype=np.int64) - LAGS // 2
    bins = lowest_bin + np.arange(freq, dtype=np.int64)
    theta = np.mod(bins[:, None] * shifts[None, :], window_samples) * (2.0 * math.pi / window_samples)
    table = np.zeros((2, 2, 2, devs, room, LAGS), np.float32)
    for kind, values in enumerate((np.cos(theta), -np.sin(theta))):
        values = values.reshape(PACK, devs, slots, LAGS)[:, :, start : start + count]
        for b in range(PACK):
            table[kind, b % 2, b // 2, :, :count] = values[b]
    table = table.reshape(-1, LAGS)
    high = table.astype(ml_dtypes.bfloat16)
    low = (table - high.astype(np.float32)).astype(ml_dtypes.bfloat16)
    return high, low


def join_kernel(*refs):
    pass


def join(token, arrays):
    anywhere = pl.BlockSpec(memory_space=pl.ANY)
    return pl.pallas_call(
        join_kernel,
        in_specs=[anywhere] * (1 + len(arrays)),
        out_specs=anywhere,
        out_shape=jax.ShapeDtypeStruct(token.shape, token.dtype),
        input_output_aliases={0: 0},
        cost_estimate=cost(0.1),
        name="join",
    )(token, *arrays)


def body(spectra, valid, source_block):
    kinds, win_dev, chans, freq = spectra.shape
    devs = lax.axis_size("win")
    stations = lax.axis_size("chan")
    groups = source_block.shape[0]
    slots = freq // PACK // devs
    sizes = chunk_sizes(slots)
    rows_out = SRC_W // devs
    windows = win_dev * devs
    own_first = stations == groups == 4
    params = pltpu.CompilerParams(vmem_limit_bytes=VMEM)

    packed = pl.pallas_call(
        functools.partial(pack_kernel, sizes, devs),
        out_shape=[
            jax.ShapeDtypeStruct((devs, n + (i == 0), chans, 128), jnp.bfloat16) for i, n in enumerate(sizes)
        ],
        scratch_shapes=[
            pltpu.VMEM((freq // 128, kinds * win_dev * chans, 128), jnp.float32),
            pltpu.VMEM((freq // PACK * chans, 128), jnp.float32),
        ],
        compiler_params=params,
        cost_estimate=cost(5),
        name="pack",
    )(spectra, valid)

    me = lax.axis_index("chan")
    if own_first:
        held = lax.rem(me - jnp.arange(groups, dtype=jnp.int32) + stations, stations)
        pos = jnp.argmax(source_block[None, :] == held[:, None], axis=1).astype(jnp.int32)
    else:
        pos = jnp.arange(groups, dtype=jnp.int32)

    me_win = lax.axis_index("win")
    per_group = chans // rows_out
    target = me_win ^ jnp.arange(devs, dtype=jnp.int32)
    holder = jnp.argmax(pos[None, :] == (target // per_group)[:, None], axis=1).astype(jnp.int32)
    row_table = holder * chans + target % per_group * rows_out

    ring = [(i, (i + 1) % stations) for i in range(stations)]
    count = len(sizes)

    def cross_call(i, token, got, heads):
        n = sizes[i]
        rows = groups * chans if own_first else (groups + 1) * chans
        half = win_dev * devs
        last = sizes[0]
        whole = pl.BlockSpec((devs, n + (i == 0), chans, 128), lambda s: (0, 0, 0, 0))
        tail = pl.BlockSpec((devs, 1, chans, 128), lambda s: (0, last, 0, 0))
        shape = (n * ROWS, rows_out, 128)
        return pl.pallas_call(
            functools.partial(cross_kernel, groups, own_first),
            grid=(1,),
            in_specs=[pl.BlockSpec(memory_space=pltpu.SMEM)] + [whole] * len(got) + [tail] * len(got),
            out_specs=[pl.BlockSpec(shape, lambda s: (0, 0, 0))] * devs,
            out_shape=[jax.ShapeDtypeStruct(shape, jnp.float32)] * devs,
            scratch_shapes=[
                pltpu.VMEM((rows, half), jnp.float32),
                pltpu.VMEM((rows, half), jnp.float32),
                pltpu.VMEM((PACK, groups * chans, 2 * half), jnp.bfloat16),
                pltpu.VMEM((PACK, groups * chans, 2 * half), jnp.bfloat16),
                pltpu.VMEM((PACK, 4 * chans, 2 * half), jnp.bfloat16),
                pltpu.VMEM((PACK, 8 * chans, 2 * half), jnp.bfloat16),
                pltpu.VMEM((groups * chans, 128), jnp.float32),
                pltpu.VMEM((ROWS, groups * chans, 128), jnp.float32),
            ],
            compiler_params=params,
            cost_estimate=cost(2 + n),
            name="cross",
        )(token, *got, *heads)

    def send_back(outs):
        back = [outs[0]] * devs
        for m in range(devs - 1, 0, -1):
            back[m] = lax.ppermute(outs[m], "win", [(d, d ^ m) for d in range(devs)])
        return back

    backs = [None] * count
    if own_first:
        back_ring = [(i, (i - 1) % stations) for i in range(stations)]
        held = {}
        crossed = {}

        def enter(i, after):
            block = join(packed[i], after) if after else packed[i]
            held[i] = [lax.all_to_all(block, "win", 0, 0, tiled=True)]

        def spread(i, after):
            own = join(held[i][0], after) if after else held[i][0]
            up = lax.ppermute(own, "chan", ring)
            down = lax.ppermute(own, "chan", back_ring)
            held[i] = [own, up, lax.ppermute(up, "chan", ring), down]

        def cross_chunk(i, after):
            token = join(row_table, after) if after else row_table
            crossed[i] = cross_call(i, token, held[i], held[0])
            backs[i] = send_back(crossed[i])

        enter(0, [])
        for i in range(count + 1):
            if i < count:
                after = []
                if i and W_Z:
                    after.append(held[i - 1][3])
                if i > 1 and W_X:
                    after.append(crossed[i - 2][0])
                spread(i, after)
                if i + 1 < count:
                    enter(i + 1, [held[max(i - 1, 0)][0 if i == 0 else 1]] if W_IN else [])
            if i:
                cross_chunk(i - 1, [backs[i - 2][-1]] if W_O and i > 1 else [])
    else:
        gathered = []
        for p in packed:
            mine = lax.all_to_all(p, "win", 0, 0, tiled=True)
            every = lax.all_gather(mine, "chan")
            picked = [lax.dynamic_index_in_dim(every, source_block[g], 0, False) for g in range(groups)]
            gathered.append(picked + [mine])
        for i in range(count):
            backs[i] = send_back(cross_call(i, row_table, gathered[i], gathered[0]))

    tile = 256
    result = []
    whole_out = jax.ShapeDtypeStruct((rows_out, chans, LAGS), jnp.float32)
    out_spec = pl.BlockSpec((rows_out, chans, tile), lambda s: (0, 0, s))
    start = 0
    for i, n in enumerate(sizes):
        pieces = [back.reshape(-1, 128) for back in backs[i]]
        high, low = lag_table(freq, devs, start, n)
        table_spec = pl.BlockSpec((high.shape[0], tile), lambda s: (0, s))
        result = pl.pallas_call(
            functools.partial(lag_kernel, n, devs, rows_out, windows, freq, len(pieces), i == 0),
            grid=(LAGS // tile,),
            in_specs=[pl.BlockSpec(memory_space=pltpu.SMEM)] + [pl.BlockSpec(pieces[0].shape, lambda s: (0, 0))] * len(pieces)
            + [table_spec] * 2
            + [out_spec] * len(result),
            out_specs=[out_spec] * 2,
            out_shape=[whole_out] * 2,
            scratch_shapes=[
                pltpu.VMEM((2 * 128, 128), jnp.float32),
                pltpu.VMEM((2 * rows_out * chans, high.shape[0]), jnp.bfloat16),
                pltpu.VMEM((2 * rows_out * chans, high.shape[0]), jnp.bfloat16),
            ],
            compiler_params=params,
            cost_estimate=cost(6),
            name="lag",
        )(me_win.reshape(1), *pieces, jnp.asarray(high), jnp.asarray(low), *result)
        start += n
    return result


def solution(mesh):
    placed = (P(None, "win", "chan", None), P("win", "chan"), P())
    return jax.shard_map(
        body,
        mesh=mesh,
        in_specs=placed,
        out_specs=(P("win", "chan", None), P("win", "chan", None)),
        check_vma=False,
    )
```

```python
import functools
import math

import jax
import jax.numpy as jnp
import ml_dtypes
import numpy as np
from jax import lax
from jax.experimental import pallas as pl
from jax.experimental.pallas import tpu as pltpu
from jax.sharding import PartitionSpec as P

LAGS = 1024
SRC_W = 128

lowest_bin = 60
window_samples = 15000
amp_eps = 1e-05
phase_floor = 0.5

ROWS = 3
PACK = 4
CHUNKS = (1 / 2, 1 / 2)
W_IN = 0
W_Z = 1
W_X = 1
W_O = 0
VMEM = 24 * 1024 * 1024


def cost(micros):
    return pl.CostEstimate(flops=0, bytes_accessed=int(micros * 3.0e6), transcendentals=0)


def chunk_sizes(slots):
    edges = [0]
    total = 0.0
    for share in CHUNKS:
        total += share
        edges.append(round(slots * total))
    return [edges[i + 1] - edges[i] for i in range(len(CHUNKS))]


def pack_kernel(sizes, devs, spectra_ref, valid_ref, *rest):
    outs, (wide, turned) = rest[: len(sizes)], rest[len(sizes) :]
    kinds, windows, chans, freq = spectra_ref.shape
    span = freq // PACK
    slots = span // devs
    real_part = spectra_ref[0].astype(jnp.float32)
    imag_part = spectra_ref[1].astype(jnp.float32)
    for i in range(freq // 128):
        cut = slice(i * 128, (i + 1) * 128)
        wide[i, pl.ds(0, windows * chans), :] = real_part[:, :, cut].reshape(windows * chans, 128)
        wide[i, pl.ds(windows * chans, windows * chans), :] = imag_part[:, :, cut].reshape(windows * chans, 128)
    total = jnp.sum(real_part * real_part + imag_part * imag_part, axis=-1, keepdims=True)
    mask = jnp.concatenate([valid_ref[...].astype(jnp.float32)] * (128 // windows), axis=0).T
    lane = lax.broadcasted_iota(jnp.int32, (chans, 128), 1)
    energy = jnp.zeros((chans, 128), jnp.float32)
    for w in range(windows):
        energy = jnp.where(lane % windows == w, total[w], energy)
    scale = mask / jnp.sqrt(energy * (1.0 / freq) + amp_eps)
    high = scale.astype(jnp.bfloat16).astype(jnp.float32)
    middle = (scale - high).astype(jnp.bfloat16).astype(jnp.float32)
    low = scale - high - middle
    part = lane // windows
    split = jnp.where(part == 0, high, jnp.where(part == 1, middle, jnp.where(part == 2, low, 0.0)))
    for c in range(chans):
        rows = []
        for k in range(kinds):
            rows_at = pl.ds(k * windows * chans + c, windows, stride=chans)
            line = jnp.concatenate([wide[i, rows_at, :] for i in range(freq // 128)], axis=1)
            for b in range(PACK):
                moved = line if b == 0 else pltpu.roll(line, freq - b * span, 1)
                rows.append(moved[:, :128])
        flipped = jnp.concatenate(rows, axis=0).T
        turned[pl.ds(c, span, stride=chans), :] = flipped[:span]
    for d in range(devs):
        start = d * slots
        for i, out in enumerate(outs):
            block = turned[pl.ds(start * chans, sizes[i] * chans), :]
            out[d, : sizes[i]] = block.astype(jnp.bfloat16).reshape(sizes[i], chans, 128)
            if i == 0:
                out[d, sizes[0]] = split.astype(jnp.bfloat16)
            start += sizes[i]


def swap_blocks(arrays, width):
    arrays = list(arrays)
    lane = lax.broadcasted_iota(jnp.int32, arrays[0].shape, 1)
    bit = 1
    while bit < len(arrays):
        upper = (lane // (width * bit)) % 2 == 1
        for i in range(len(arrays)):
            if i & bit == 0:
                a, c = arrays[i], arrays[i | bit]
                arrays[i] = jnp.where(upper, pltpu.roll(c, width * bit, 1), a)
                arrays[i | bit] = jnp.where(upper, c, pltpu.roll(a, 128 - width * bit, 1))
        bit *= 2
    return arrays


def cross_kernel(groups, own_first, first, rows_ref, *rest):
    blocks = rest[:groups]
    rest = rest[groups:]
    own = blocks[0]
    if not own_first:
        own, rest = rest[0], rest[1:]
    if first:
        count = groups + (not own_first)
        scale_refs, rest = rest[:count], rest[count:]
    else:
        (factor, cap, inv), rest = rest[:3], rest[3:]
    devs, chans = own.shape[0], own.shape[2]
    outs, rest = rest[:devs], rest[devs:]
    if first:
        (factor, cap, inv), rest = rest[:3], rest[3:]
    src_white, src_unit, recv_white, recv_unit, packed = rest
    width = 128 // 8
    parts = devs // 8
    half = parts * 128
    slots = outs[0].shape[0] // ROWS
    rows_out = outs[0].shape[1]

    def opened(ref, q, part):
        moved = swap_blocks([ref[part * 8 + d, q] for d in range(8)], width)
        return [block.astype(jnp.float32) for block in moved]

    if first:
        for g, ref in enumerate(scale_refs):
            for part in range(parts):
                got = opened(ref, 0, part)
                value = got[0] + got[1] + got[2]
                factor[pl.ds(g * chans, chans), pl.ds(part * 128, 128)] = value
                cap[pl.ds(g * chans, chans), pl.ds(part * 128, 128)] = jnp.where(value > 0, 1.0 / phase_floor, 0.0)
        masks = jnp.where(cap[...] > 0, 1.0, 0.0).astype(jnp.bfloat16)
        mine = 0 if own_first else groups * chans
        recv = jnp.concatenate([masks[mine : mine + chans]] * 4, axis=0)
        counts = lax.dot_general(
            masks[: groups * chans], recv, (((1,), (1,)), ((), ())), preferred_element_type=jnp.float32
        )
        inv[...] = 1.0 / jnp.maximum(counts, 1.0)
    data_refs = list(blocks) if own_first else list(blocks) + [own]

    def step(q, carry):
        for g, ref in enumerate(data_refs):
            rows = pl.ds(g * chans, chans)
            for part in range(parts):
                got = opened(ref, q, part)
                scale = factor[rows, pl.ds(part * 128, 128)]
                limit = cap[rows, pl.ds(part * 128, 128)]
                lo = pl.ds(part * 128, 128)
                hi = pl.ds(half + part * 128, 128)
                for b in range(PACK):
                    real_part, imag_part = got[b], got[PACK + b]
                    power = real_part * real_part + imag_part * imag_part
                    phase = jnp.minimum(lax.rsqrt(power), limit)
                    white_re = (real_part * scale).astype(jnp.bfloat16)
                    white_im = (imag_part * scale).astype(jnp.bfloat16)
                    unit_re = (real_part * phase).astype(jnp.bfloat16)
                    unit_im = (imag_part * phase).astype(jnp.bfloat16)
                    if g < groups:
                        src_white[b, rows, lo] = white_re
                        src_white[b, rows, hi] = white_im
                        src_unit[b, rows, lo] = unit_re
                        src_unit[b, rows, hi] = unit_im
                    if g == (0 if own_first else groups):
                        for t in range(4):
                            at = pl.ds(t * chans, chans)
                            recv_white[b, at, lo] = white_im if t % 2 else white_re
                            recv_white[b, at, hi] = -white_re if t % 2 else white_im
                        for t in range(8):
                            at = pl.ds(t * chans, chans)
                            odd = (t + t // 4) % 2
                            recv_unit[b, at, lo] = unit_im if odd else unit_re
                            recv_unit[b, at, hi] = -unit_re if odd else unit_im
        scaled = inv[...]
        lane = lax.broadcasted_iota(jnp.int32, scaled.shape, 1)
        means, cohers = [], []
        for b in range(PACK):
            lin = lax.dot_general(
                src_white[b], recv_white[b], (((1,), (1,)), ((), ())), preferred_element_type=jnp.float32
            )
            pha = lax.dot_general(
                src_unit[b], recv_unit[b], (((1,), (1,)), ((), ())), preferred_element_type=jnp.float32
            )
            means.append(lin * scaled)
            one = pha[:, :128] * scaled
            two = pha[:, 128:] * scaled
            cohers.append(one * one + two * two)
        packed[0] = jnp.where(lane < 2 * chans, means[0], means[1])
        packed[1] = jnp.where(lane < 2 * chans, means[2], means[3])
        low = jnp.where(lane < chans, cohers[0], cohers[1])
        high = jnp.where(lane < 3 * chans, cohers[2], cohers[3])
        packed[2] = jnp.where(lane < 2 * chans, low, high)
        for m, out in enumerate(outs):
            at = pl.ds(pl.multiple_of(rows_ref[m], rows_out), rows_out)
            for t in range(ROWS):
                out[q * ROWS + t] = packed[t, at, :]
        return carry

    lax.fori_loop(0, slots, step, 0, unroll=3)


def lag_kernel(slots, devs, rows_out, windows, freq, pieces, first, me_ref, *rest):
    refs, rest = rest[:pieces], rest[pieces:]
    table_high, table_low, rest = rest[0], rest[1], rest[2:]
    if not first:
        linear_before, weighted_before, rest = rest[0], rest[1], rest[2:]
    linear, weighted, staged, left_high, left_low = rest
    chans = linear.shape[1]
    side = 128 // 2
    room = side // devs
    factor = math.sqrt(windows / freq)

    @pl.when(pl.program_id(0) == 0)
    def fill():
        def store(rows, value):
            high = value.astype(jnp.bfloat16)
            left_high[rows, :] = high
            left_low[rows, :] = (value - high.astype(jnp.float32)).astype(jnp.bfloat16)

        pad = jnp.zeros((max(room - slots, 1), 128), jnp.float32)
        lane = lax.broadcasted_iota(jnp.int32, (chans, 128), 1)
        for s in range(rows_out):
            for m in range(devs):
                at = pl.multiple_of((me_ref[0] ^ m) * room, room)
                for t, places in enumerate(((0,), (1,), (2, 3))):
                    block = refs[m][pl.ds(t * rows_out + s, slots, stride=ROWS * rows_out), :]
                    block = jnp.concatenate([block, pad], axis=0) if room > slots else block
                    for place in places:
                        staged[pl.ds(place * side + at, room), :] = block
            means = staged[: 2 * side].T * factor
            coher = staged[2 * side :].T * windows
            blocks = [coher[b * chans : (b + 1) * chans] for b in range(PACK)]
            weights = [jnp.where(lane < side, blocks[0], blocks[2]), jnp.where(lane < side, blocks[1], blocks[3])]
            parts = [means[i * chans : (i + 1) * chans] for i in range(4)]
            plain = [parts[0], parts[2], parts[1], parts[3]]
            store(pl.ds(s * chans, chans), jnp.concatenate(plain, axis=1))
            scaled = [part * weights[i % 2] for i, part in enumerate(plain)]
            store(pl.ds((rows_out + s) * chans, chans), jnp.concatenate(scaled, axis=1))

    total = jnp.dot(left_high[...], table_high[...], preferred_element_type=jnp.float32)
    total += jnp.dot(left_high[...], table_low[...], preferred_element_type=jnp.float32)
    total += jnp.dot(left_low[...], table_high[...], preferred_element_type=jnp.float32)
    half = rows_out * chans
    for out, share, before in (
        (linear, total[:half], None if first else linear_before),
        (weighted, total[half:], None if first else weighted_before),
    ):
        share = share.reshape(out.shape)
        out[...] = share if first else share + before[...]


def lag_table(freq, devs, start, count):
    span = freq // PACK
    slots = span // devs
    room = 128 // 2 // devs
    shifts = np.arange(LAGS, dtype=np.int64) - LAGS // 2
    bins = lowest_bin + np.arange(freq, dtype=np.int64)
    theta = np.mod(bins[:, None] * shifts[None, :], window_samples) * (2.0 * math.pi / window_samples)
    table = np.zeros((2, 2, 2, devs, room, LAGS), np.float32)
    for kind, values in enumerate((np.cos(theta), -np.sin(theta))):
        values = values.reshape(PACK, devs, slots, LAGS)[:, :, start : start + count]
        for b in range(PACK):
            table[kind, b % 2, b // 2, :, :count] = values[b]
    table = table.reshape(-1, LAGS)
    high = table.astype(ml_dtypes.bfloat16)
    low = (table - high.astype(np.float32)).astype(ml_dtypes.bfloat16)
    return high, low


def join_kernel(*refs):
    pass


def join(token, arrays):
    anywhere = pl.BlockSpec(memory_space=pl.ANY)
    return pl.pallas_call(
        join_kernel,
        in_specs=[anywhere] * (1 + len(arrays)),
        out_specs=anywhere,
        out_shape=jax.ShapeDtypeStruct(token.shape, token.dtype),
        input_output_aliases={0: 0},
        cost_estimate=cost(0.1),
        name="join",
    )(token, *arrays)


def body(spectra, valid, source_block):
    kinds, win_dev, chans, freq = spectra.shape
    devs = lax.axis_size("win")
    stations = lax.axis_size("chan")
    groups = source_block.shape[0]
    slots = freq // PACK // devs
    sizes = chunk_sizes(slots)
    rows_out = SRC_W // devs
    windows = win_dev * devs
    own_first = stations == groups == 4
    params = pltpu.CompilerParams(vmem_limit_bytes=VMEM)

    packed = pl.pallas_call(
        functools.partial(pack_kernel, sizes, devs),
        out_shape=[
            jax.ShapeDtypeStruct((devs, n + (i == 0), chans, 128), jnp.bfloat16) for i, n in enumerate(sizes)
        ],
        scratch_shapes=[
            pltpu.VMEM((freq // 128, kinds * win_dev * chans, 128), jnp.float32),
            pltpu.VMEM((freq // PACK * chans, 128), jnp.float32),
        ],
        compiler_params=params,
        cost_estimate=cost(5),
        name="pack",
    )(spectra, valid)

    me = lax.axis_index("chan")
    if own_first:
        held = lax.rem(me - jnp.arange(groups, dtype=jnp.int32) + stations, stations)
        pos = jnp.argmax(source_block[None, :] == held[:, None], axis=1).astype(jnp.int32)
    else:
        pos = jnp.arange(groups, dtype=jnp.int32)

    me_win = lax.axis_index("win")
    per_group = chans // rows_out
    target = me_win ^ jnp.arange(devs, dtype=jnp.int32)
    holder = jnp.argmax(pos[None, :] == (target // per_group)[:, None], axis=1).astype(jnp.int32)
    row_table = holder * chans + target % per_group * rows_out

    ring = [(i, (i + 1) % stations) for i in range(stations)]
    count = len(sizes)

    shared = []

    def cross_call(i, token, got, heads):
        n = sizes[i]
        rows = groups * chans if own_first else (groups + 1) * chans
        half = win_dev * devs
        last = sizes[0]
        first = i == 0
        whole = pl.BlockSpec((devs, n + first, chans, 128), lambda s: (0, 0, 0, 0))
        shape = (n * ROWS, rows_out, 128)
        flat = lambda s: (0, 0)
        tables = [(rows, half), (rows, half), (groups * chans, 128)]
        table_specs = [pl.BlockSpec(t, flat) for t in tables]
        out_specs = [pl.BlockSpec(shape, lambda s: (0, 0, 0))] * devs
        out_shape = [jax.ShapeDtypeStruct(shape, jnp.float32)] * devs
        if first:
            extra = list(heads)
            extra_specs = [pl.BlockSpec((devs, 1, chans, 128), lambda s: (0, last, 0, 0))] * len(heads)
            out_specs = out_specs + table_specs
            out_shape = out_shape + [jax.ShapeDtypeStruct(t, jnp.float32) for t in tables]
        else:
            extra, extra_specs = list(shared), table_specs
        result = pl.pallas_call(
            functools.partial(cross_kernel, groups, own_first, first),
            grid=(1,),
            in_specs=[pl.BlockSpec(memory_space=pltpu.SMEM)] + [whole] * len(got) + extra_specs,
            out_specs=out_specs,
            out_shape=out_shape,
            scratch_shapes=[
                pltpu.VMEM((PACK, groups * chans, 2 * half), jnp.bfloat16),
                pltpu.VMEM((PACK, groups * chans, 2 * half), jnp.bfloat16),
                pltpu.VMEM((PACK, 4 * chans, 2 * half), jnp.bfloat16),
                pltpu.VMEM((PACK, 8 * chans, 2 * half), jnp.bfloat16),
                pltpu.VMEM((ROWS, groups * chans, 128), jnp.float32),
            ],
            compiler_params=params,
            cost_estimate=cost(1 + first + n),
            name="cross",
        )(token, *got, *extra)
        if first:
            shared.extend(result[devs:])
        return result[:devs]

    def send_back(outs):
        back = [outs[0]] * devs
        for m in range(devs - 1, 0, -1):
            back[m] = lax.ppermute(outs[m], "win", [(d, d ^ m) for d in range(devs)])
        return back

    backs = [None] * count
    if own_first:
        back_ring = [(i, (i - 1) % stations) for i in range(stations)]
        held = {}
        crossed = {}

        def enter(i, after):
            block = join(packed[i], after) if after else packed[i]
            held[i] = [lax.all_to_all(block, "win", 0, 0, tiled=True)]

        def spread(i, after):
            own = join(held[i][0], after) if after else held[i][0]
            up = lax.ppermute(own, "chan", ring)
            down = lax.ppermute(own, "chan", back_ring)
            held[i] = [own, up, lax.ppermute(up, "chan", ring), down]

        def cross_chunk(i, after):
            token = join(row_table, after) if after else row_table
            crossed[i] = cross_call(i, token, held[i], held[0])
            backs[i] = send_back(crossed[i])

        enter(0, [])
        for i in range(count + 1):
            if i < count:
                after = []
                if i and W_Z:
                    after.append(held[i - 1][3])
                if i > 1 and W_X:
                    after.append(crossed[i - 2][0])
                spread(i, after)
                if i + 1 < count:
                    enter(i + 1, [held[max(i - 1, 0)][0 if i == 0 else 1]] if W_IN else [])
            if i:
                cross_chunk(i - 1, [backs[i - 2][-1]] if W_O and i > 1 else [])
    else:
        gathered = []
        for p in packed:
            mine = lax.all_to_all(p, "win", 0, 0, tiled=True)
            every = lax.all_gather(mine, "chan")
            picked = [lax.dynamic_index_in_dim(every, source_block[g], 0, False) for g in range(groups)]
            gathered.append(picked + [mine])
        for i in range(count):
            backs[i] = send_back(cross_call(i, row_table, gathered[i], gathered[0]))

    tile = 256
    result = []
    whole_out = jax.ShapeDtypeStruct((rows_out, chans, LAGS), jnp.float32)
    out_spec = pl.BlockSpec((rows_out, chans, tile), lambda s: (0, 0, s))
    start = 0
    for i, n in enumerate(sizes):
        pieces = [back.reshape(-1, 128) for back in backs[i]]
        high, low = lag_table(freq, devs, start, n)
        table_spec = pl.BlockSpec((high.shape[0], tile), lambda s: (0, s))
        result = pl.pallas_call(
            functools.partial(lag_kernel, n, devs, rows_out, windows, freq, len(pieces), i == 0),
            grid=(LAGS // tile,),
            in_specs=[pl.BlockSpec(memory_space=pltpu.SMEM)] + [pl.BlockSpec(pieces[0].shape, lambda s: (0, 0))] * len(pieces)
            + [table_spec] * 2
            + [out_spec] * len(result),
            out_specs=[out_spec] * 2,
            out_shape=[whole_out] * 2,
            scratch_shapes=[
                pltpu.VMEM((2 * 128, 128), jnp.float32),
                pltpu.VMEM((2 * rows_out * chans, high.shape[0]), jnp.bfloat16),
                pltpu.VMEM((2 * rows_out * chans, high.shape[0]), jnp.bfloat16),
            ],
            compiler_params=params,
            cost_estimate=cost(6),
            name="lag",
        )(me_win.reshape(1), *pieces, jnp.asarray(high), jnp.asarray(low), *result)
        start += n
    return result


def solution(mesh):
    placed = (P(None, "win", "chan", None), P("win", "chan"), P())
    return jax.shard_map(
        body,
        mesh=mesh,
        in_specs=placed,
        out_specs=(P("win", "chan", None), P("win", "chan", None)),
        check_vma=False,
    )
```

```python
import functools
import math

import jax
import jax.numpy as jnp
import ml_dtypes
import numpy as np
from jax import lax
from jax.experimental import pallas as pl
from jax.experimental.pallas import tpu as pltpu
from jax.sharding import PartitionSpec as P

LAGS = 1024
SRC_W = 128

lowest_bin = 60
window_samples = 15000
amp_eps = 1e-05
phase_floor = 0.5

ROWS = 3
PACK = 4
CHUNKS = (1 / 2, 1 / 2)
W_IN = 0
W_Z = 1
W_X = 1
W_O = 0
VMEM = 36 * 1024 * 1024


def cost(micros):
    return pl.CostEstimate(flops=0, bytes_accessed=int(micros * 3.0e6), transcendentals=0)


def chunk_sizes(slots):
    edges = [0]
    total = 0.0
    for share in CHUNKS:
        total += share
        edges.append(round(slots * total))
    return [edges[i + 1] - edges[i] for i in range(len(CHUNKS))]


def pack_kernel(sizes, devs, spectra_ref, valid_ref, *rest):
    outs, (wide, turned) = rest[: len(sizes)], rest[len(sizes) :]
    kinds, windows, chans, freq = spectra_ref.shape
    span = freq // PACK
    slots = span // devs
    real_part = spectra_ref[0].astype(jnp.float32)
    imag_part = spectra_ref[1].astype(jnp.float32)
    for i in range(freq // 128):
        cut = slice(i * 128, (i + 1) * 128)
        wide[i, pl.ds(0, windows * chans), :] = real_part[:, :, cut].reshape(windows * chans, 128)
        wide[i, pl.ds(windows * chans, windows * chans), :] = imag_part[:, :, cut].reshape(windows * chans, 128)
    total = jnp.sum(real_part * real_part + imag_part * imag_part, axis=-1, keepdims=True)
    mask = jnp.concatenate([valid_ref[...].astype(jnp.float32)] * (128 // windows), axis=0).T
    lane = lax.broadcasted_iota(jnp.int32, (chans, 128), 1)
    energy = jnp.zeros((chans, 128), jnp.float32)
    for w in range(windows):
        energy = jnp.where(lane % windows == w, total[w], energy)
    scale = mask / jnp.sqrt(energy * (1.0 / freq) + amp_eps)
    high = scale.astype(jnp.bfloat16).astype(jnp.float32)
    middle = (scale - high).astype(jnp.bfloat16).astype(jnp.float32)
    low = scale - high - middle
    part = lane // windows
    split = jnp.where(part == 0, high, jnp.where(part == 1, middle, jnp.where(part == 2, low, 0.0)))
    for c in range(chans):
        rows = []
        for k in range(kinds):
            rows_at = pl.ds(k * windows * chans + c, windows, stride=chans)
            line = jnp.concatenate([wide[i, rows_at, :] for i in range(freq // 128)], axis=1)
            for b in range(PACK):
                moved = line if b == 0 else pltpu.roll(line, freq - b * span, 1)
                rows.append(moved[:, :128])
        flipped = jnp.concatenate(rows, axis=0).T
        turned[pl.ds(c, span, stride=chans), :] = flipped[:span]
    for d in range(devs):
        start = d * slots
        for i, out in enumerate(outs):
            block = turned[pl.ds(start * chans, sizes[i] * chans), :]
            out[d, : sizes[i]] = block.astype(jnp.bfloat16).reshape(sizes[i], chans, 128)
            if i == 0:
                out[d, sizes[0]] = split.astype(jnp.bfloat16)
            start += sizes[i]


def swap_blocks(arrays, width):
    arrays = list(arrays)
    lane = lax.broadcasted_iota(jnp.int32, arrays[0].shape, 1)
    bit = 1
    while bit < len(arrays):
        upper = (lane // (width * bit)) % 2 == 1
        for i in range(len(arrays)):
            if i & bit == 0:
                a, c = arrays[i], arrays[i | bit]
                arrays[i] = jnp.where(upper, pltpu.roll(c, width * bit, 1), a)
                arrays[i | bit] = jnp.where(upper, c, pltpu.roll(a, 128 - width * bit, 1))
        bit *= 2
    return arrays


def cross_kernel(groups, own_first, first, rows_ref, *rest):
    blocks = rest[:groups]
    rest = rest[groups:]
    own = blocks[0]
    if not own_first:
        own, rest = rest[0], rest[1:]
    if first:
        count = groups + (not own_first)
        scale_refs, rest = rest[:count], rest[count:]
    else:
        (factor, cap, inv), rest = rest[:3], rest[3:]
    devs, chans = own.shape[0], own.shape[2]
    outs, rest = rest[:devs], rest[devs:]
    if first:
        (factor, cap, inv), rest = rest[:3], rest[3:]
    src_white, src_unit, recv_white, recv_unit, packed = rest
    width = 128 // 8
    parts = devs // 8
    half = parts * 128
    slots = outs[0].shape[0] // ROWS
    rows_out = outs[0].shape[1]

    def opened(ref, q, part):
        moved = swap_blocks([ref[part * 8 + d, q] for d in range(8)], width)
        return [block.astype(jnp.float32) for block in moved]

    if first:
        for g, ref in enumerate(scale_refs):
            for part in range(parts):
                got = opened(ref, 0, part)
                value = got[0] + got[1] + got[2]
                factor[pl.ds(g * chans, chans), pl.ds(part * 128, 128)] = value
                cap[pl.ds(g * chans, chans), pl.ds(part * 128, 128)] = jnp.where(value > 0, 1.0 / phase_floor, 0.0)
        masks = jnp.where(cap[...] > 0, 1.0, 0.0).astype(jnp.bfloat16)
        mine = 0 if own_first else groups * chans
        recv = jnp.concatenate([masks[mine : mine + chans]] * 4, axis=0)
        counts = lax.dot_general(
            masks[: groups * chans], recv, (((1,), (1,)), ((), ())), preferred_element_type=jnp.float32
        )
        inv[...] = 1.0 / jnp.maximum(counts, 1.0)
    data_refs = list(blocks) if own_first else list(blocks) + [own]

    def step(q, carry):
        for g, ref in enumerate(data_refs):
            rows = pl.ds(g * chans, chans)
            for part in range(parts):
                got = opened(ref, q, part)
                scale = factor[rows, pl.ds(part * 128, 128)]
                limit = cap[rows, pl.ds(part * 128, 128)]
                lo = pl.ds(part * 128, 128)
                hi = pl.ds(half + part * 128, 128)
                for b in range(PACK):
                    real_part, imag_part = got[b], got[PACK + b]
                    power = real_part * real_part + imag_part * imag_part
                    phase = jnp.minimum(lax.rsqrt(power), limit)
                    white_re = (real_part * scale).astype(jnp.bfloat16)
                    white_im = (imag_part * scale).astype(jnp.bfloat16)
                    unit_re = (real_part * phase).astype(jnp.bfloat16)
                    unit_im = (imag_part * phase).astype(jnp.bfloat16)
                    if g < groups:
                        src_white[b, rows, lo] = white_re
                        src_white[b, rows, hi] = white_im
                        src_unit[b, rows, lo] = unit_re
                        src_unit[b, rows, hi] = unit_im
                    if g == (0 if own_first else groups):
                        for t in range(4):
                            at = pl.ds(t * chans, chans)
                            recv_white[b, at, lo] = white_im if t % 2 else white_re
                            recv_white[b, at, hi] = -white_re if t % 2 else white_im
                        for t in range(8):
                            at = pl.ds(t * chans, chans)
                            odd = (t + t // 4) % 2
                            recv_unit[b, at, lo] = unit_im if odd else unit_re
                            recv_unit[b, at, hi] = -unit_re if odd else unit_im
        scaled = inv[...]
        lane = lax.broadcasted_iota(jnp.int32, scaled.shape, 1)
        means, cohers = [], []
        for b in range(PACK):
            lin = lax.dot_general(
                src_white[b], recv_white[b], (((1,), (1,)), ((), ())), preferred_element_type=jnp.float32
            )
            pha = lax.dot_general(
                src_unit[b], recv_unit[b], (((1,), (1,)), ((), ())), preferred_element_type=jnp.float32
            )
            means.append(lin * scaled)
            one = pha[:, :128] * scaled
            two = pha[:, 128:] * scaled
            cohers.append(one * one + two * two)
        packed[0] = jnp.where(lane < 2 * chans, means[0], means[1])
        packed[1] = jnp.where(lane < 2 * chans, means[2], means[3])
        low = jnp.where(lane < chans, cohers[0], cohers[1])
        high = jnp.where(lane < 3 * chans, cohers[2], cohers[3])
        packed[2] = jnp.where(lane < 2 * chans, low, high)
        for m, out in enumerate(outs):
            at = pl.ds(pl.multiple_of(rows_ref[m], rows_out), rows_out)
            for t in range(ROWS):
                out[q * ROWS + t] = packed[t, at, :]
        return carry

    lax.fori_loop(0, slots, step, 0, unroll=3)


def lag_kernel(slots, devs, rows_out, windows, freq, pieces, first, me_ref, *rest):
    refs, rest = rest[:pieces], rest[pieces:]
    table_high, table_low, rest = rest[0], rest[1], rest[2:]
    if not first:
        linear_before, weighted_before, rest = rest[0], rest[1], rest[2:]
    linear, weighted, staged, left_high, left_low = rest
    chans = linear.shape[1]
    side = 128 // 2
    room = side // devs
    factor = math.sqrt(windows / freq)

    @pl.when(pl.program_id(0) == 0)
    def fill():
        def store(rows, value):
            high = value.astype(jnp.bfloat16)
            left_high[rows, :] = high
            left_low[rows, :] = (value - high.astype(jnp.float32)).astype(jnp.bfloat16)

        pad = jnp.zeros((max(room - slots, 1), 128), jnp.float32)
        lane = lax.broadcasted_iota(jnp.int32, (chans, 128), 1)
        for s in range(rows_out):
            for m in range(devs):
                at = pl.multiple_of((me_ref[0] ^ m) * room, room)
                for t, places in enumerate(((0,), (1,), (2, 3))):
                    block = refs[m][pl.ds(t * rows_out + s, slots, stride=ROWS * rows_out), :]
                    block = jnp.concatenate([block, pad], axis=0) if room > slots else block
                    for place in places:
                        staged[pl.ds(place * side + at, room), :] = block
            means = staged[: 2 * side].T * factor
            coher = staged[2 * side :].T * windows
            blocks = [coher[b * chans : (b + 1) * chans] for b in range(PACK)]
            weights = [jnp.where(lane < side, blocks[0], blocks[2]), jnp.where(lane < side, blocks[1], blocks[3])]
            parts = [means[i * chans : (i + 1) * chans] for i in range(4)]
            plain = [parts[0], parts[2], parts[1], parts[3]]
            store(pl.ds(s * chans, chans), jnp.concatenate(plain, axis=1))
            scaled = [part * weights[i % 2] for i, part in enumerate(plain)]
            store(pl.ds((rows_out + s) * chans, chans), jnp.concatenate(scaled, axis=1))

    total = jnp.dot(left_high[...], table_high[...], preferred_element_type=jnp.float32)
    total += jnp.dot(left_high[...], table_low[...], preferred_element_type=jnp.float32)
    total += jnp.dot(left_low[...], table_high[...], preferred_element_type=jnp.float32)
    half = rows_out * chans
    for out, share, before in (
        (linear, total[:half], None if first else linear_before),
        (weighted, total[half:], None if first else weighted_before),
    ):
        share = share.reshape(out.shape)
        out[...] = share if first else share + before[...]


def lag_table(freq, devs, start, count):
    span = freq // PACK
    slots = span // devs
    room = 128 // 2 // devs
    shifts = np.arange(LAGS, dtype=np.int64) - LAGS // 2
    bins = lowest_bin + np.arange(freq, dtype=np.int64)
    theta = np.mod(bins[:, None] * shifts[None, :], window_samples) * (2.0 * math.pi / window_samples)
    table = np.zeros((2, 2, 2, devs, room, LAGS), np.float32)
    for kind, values in enumerate((np.cos(theta), -np.sin(theta))):
        values = values.reshape(PACK, devs, slots, LAGS)[:, :, start : start + count]
        for b in range(PACK):
            table[kind, b % 2, b // 2, :, :count] = values[b]
    table = table.reshape(-1, LAGS)
    high = table.astype(ml_dtypes.bfloat16)
    low = (table - high.astype(np.float32)).astype(ml_dtypes.bfloat16)
    return high, low


def join_kernel(*refs):
    pass


def join(token, arrays):
    anywhere = pl.BlockSpec(memory_space=pl.ANY)
    return pl.pallas_call(
        join_kernel,
        in_specs=[anywhere] * (1 + len(arrays)),
        out_specs=anywhere,
        out_shape=jax.ShapeDtypeStruct(token.shape, token.dtype),
        input_output_aliases={0: 0},
        cost_estimate=cost(0.1),
        name="join",
    )(token, *arrays)


def body(spectra, valid, source_block):
    kinds, win_dev, chans, freq = spectra.shape
    devs = lax.axis_size("win")
    stations = lax.axis_size("chan")
    groups = source_block.shape[0]
    slots = freq // PACK // devs
    sizes = chunk_sizes(slots)
    rows_out = SRC_W // devs
    windows = win_dev * devs
    own_first = stations == groups == 4
    params = pltpu.CompilerParams(vmem_limit_bytes=VMEM)

    packed = pl.pallas_call(
        functools.partial(pack_kernel, sizes, devs),
        out_shape=[
            jax.ShapeDtypeStruct((devs, n + (i == 0), chans, 128), jnp.bfloat16) for i, n in enumerate(sizes)
        ],
        scratch_shapes=[
            pltpu.VMEM((freq // 128, kinds * win_dev * chans, 128), jnp.float32),
            pltpu.VMEM((freq // PACK * chans, 128), jnp.float32),
        ],
        compiler_params=params,
        cost_estimate=cost(5),
        name="pack",
    )(spectra, valid)

    me = lax.axis_index("chan")
    if own_first:
        held = lax.rem(me - jnp.arange(groups, dtype=jnp.int32) + stations, stations)
        pos = jnp.argmax(source_block[None, :] == held[:, None], axis=1).astype(jnp.int32)
    else:
        pos = jnp.arange(groups, dtype=jnp.int32)

    me_win = lax.axis_index("win")
    per_group = chans // rows_out
    target = me_win ^ jnp.arange(devs, dtype=jnp.int32)
    holder = jnp.argmax(pos[None, :] == (target // per_group)[:, None], axis=1).astype(jnp.int32)
    row_table = holder * chans + target % per_group * rows_out

    ring = [(i, (i + 1) % stations) for i in range(stations)]
    count = len(sizes)

    shared = []

    def cross_call(i, token, got, heads):
        n = sizes[i]
        rows = groups * chans if own_first else (groups + 1) * chans
        half = win_dev * devs
        last = sizes[0]
        first = i == 0
        whole = pl.BlockSpec((devs, n + first, chans, 128), lambda s: (0, 0, 0, 0))
        shape = (n * ROWS, rows_out, 128)
        flat = lambda s: (0, 0)
        tables = [(rows, half), (rows, half), (groups * chans, 128)]
        table_specs = [pl.BlockSpec(t, flat) for t in tables]
        out_specs = [pl.BlockSpec(shape, lambda s: (0, 0, 0))] * devs
        out_shape = [jax.ShapeDtypeStruct(shape, jnp.float32)] * devs
        if first:
            extra = list(heads)
            extra_specs = [pl.BlockSpec((devs, 1, chans, 128), lambda s: (0, last, 0, 0))] * len(heads)
            out_specs = out_specs + table_specs
            out_shape = out_shape + [jax.ShapeDtypeStruct(t, jnp.float32) for t in tables]
        else:
            extra, extra_specs = list(shared), table_specs
        result = pl.pallas_call(
            functools.partial(cross_kernel, groups, own_first, first),
            grid=(1,),
            in_specs=[pl.BlockSpec(memory_space=pltpu.SMEM)] + [whole] * len(got) + extra_specs,
            out_specs=out_specs,
            out_shape=out_shape,
            scratch_shapes=[
                pltpu.VMEM((PACK, groups * chans, 2 * half), jnp.bfloat16),
                pltpu.VMEM((PACK, groups * chans, 2 * half), jnp.bfloat16),
                pltpu.VMEM((PACK, 4 * chans, 2 * half), jnp.bfloat16),
                pltpu.VMEM((PACK, 8 * chans, 2 * half), jnp.bfloat16),
                pltpu.VMEM((ROWS, groups * chans, 128), jnp.float32),
            ],
            compiler_params=params,
            cost_estimate=cost(1 + first + n),
            name="cross",
        )(token, *got, *extra)
        if first:
            shared.extend(result[devs:])
        return result[:devs]

    def send_back(outs):
        back = [outs[0]] * devs
        for m in range(devs - 1, 0, -1):
            back[m] = lax.ppermute(outs[m], "win", [(d, d ^ m) for d in range(devs)])
        return back

    backs = [None] * count
    if own_first:
        back_ring = [(i, (i - 1) % stations) for i in range(stations)]
        held = {}
        crossed = {}

        def enter(i, after):
            block = join(packed[i], after) if after else packed[i]
            held[i] = [lax.all_to_all(block, "win", 0, 0, tiled=True)]

        def spread(i, after):
            own = join(held[i][0], after) if after else held[i][0]
            up = lax.ppermute(own, "chan", ring)
            down = lax.ppermute(own, "chan", back_ring)
            held[i] = [own, up, lax.ppermute(up, "chan", ring), down]

        def cross_chunk(i, after):
            token = join(row_table, after) if after else row_table
            crossed[i] = cross_call(i, token, held[i], held[0])
            backs[i] = send_back(crossed[i])

        enter(0, [])
        for i in range(count + 1):
            if i < count:
                after = []
                if i and W_Z:
                    after.append(held[i - 1][3])
                if i > 1 and W_X:
                    after.append(crossed[i - 2][0])
                spread(i, after)
                if i + 1 < count:
                    enter(i + 1, [held[max(i - 1, 0)][0 if i == 0 else 1]] if W_IN else [])
            if i:
                cross_chunk(i - 1, [backs[i - 2][-1]] if W_O and i > 1 else [])
    else:
        gathered = []
        for p in packed:
            mine = lax.all_to_all(p, "win", 0, 0, tiled=True)
            every = lax.all_gather(mine, "chan")
            picked = [lax.dynamic_index_in_dim(every, source_block[g], 0, False) for g in range(groups)]
            gathered.append(picked + [mine])
        for i in range(count):
            backs[i] = send_back(cross_call(i, row_table, gathered[i], gathered[0]))

    tile = 512
    result = []
    whole_out = jax.ShapeDtypeStruct((rows_out, chans, LAGS), jnp.float32)
    out_spec = pl.BlockSpec((rows_out, chans, tile), lambda s: (0, 0, s))
    start = 0
    for i, n in enumerate(sizes):
        pieces = [back.reshape(-1, 128) for back in backs[i]]
        high, low = lag_table(freq, devs, start, n)
        table_spec = pl.BlockSpec((high.shape[0], tile), lambda s: (0, s))
        result = pl.pallas_call(
            functools.partial(lag_kernel, n, devs, rows_out, windows, freq, len(pieces), i == 0),
            grid=(LAGS // tile,),
            in_specs=[pl.BlockSpec(memory_space=pltpu.SMEM)] + [pl.BlockSpec(pieces[0].shape, lambda s: (0, 0))] * len(pieces)
            + [table_spec] * 2
            + [out_spec] * len(result),
            out_specs=[out_spec] * 2,
            out_shape=[whole_out] * 2,
            scratch_shapes=[
                pltpu.VMEM((2 * 128, 128), jnp.float32),
                pltpu.VMEM((2 * rows_out * chans, high.shape[0]), jnp.bfloat16),
                pltpu.VMEM((2 * rows_out * chans, high.shape[0]), jnp.bfloat16),
            ],
            compiler_params=params,
            cost_estimate=cost(6),
            name="lag",
        )(me_win.reshape(1), *pieces, jnp.asarray(high), jnp.asarray(low), *result)
        start += n
    return result


def solution(mesh):
    placed = (P(None, "win", "chan", None), P("win", "chan"), P())
    return jax.shard_map(
        body,
        mesh=mesh,
        in_specs=placed,
        out_specs=(P("win", "chan", None), P("win", "chan", None)),
        check_vma=False,
    )
```
